512 devices in a mesh: seq: 32 (over y_lo, z), tp: 8 (over x, core), dp: 2 (over y_hi).
Axes of the slice: x: 4, y: 4 (y_hi: 2, y_lo: 2; y = y_hi * 2 + y_lo), z: 16, core: 2. Of those that a mesh axis runs over, the one named last changes fastest.
Arguments:
- hidden: bfloat16 [32768, 3072], P(('dp', 'seq'), 'tp'), parts along dimension 0, may hold values from -6 to 6
- shift_mod: float32 [6144], P('dp'), parts along dimension 0, may hold values from -3 to 3
- scale_mod: float32 [6144], P('dp'), parts along dimension 0, may hold values from -3 to 3
- gate: float32 [6144], P('dp'), parts along dimension 0, may hold values from -4 to 4
- w_qkv: bfloat16 [3072, 3, 2, 1024], P('seq', None, None, 'tp')
- w_out: bfloat16 [2, 1024, 3072], P(None, 'tp'), may hold values from -0.125 to 0.125
- window_tiles: int32 [8, 4], replicated, may hold values from 0 to 7, as said below
Outputs:
- mixed: bfloat16 [32768, 3072], P(('dp', 'seq'), 'tp'), parts along dimension 0
The draws below stay inside these ranges and needn't reach their ends.
There are 2 independent parts, one for each index of `dp`. The reference program is written for one: setup_inputs(seed, part) draws one part's arguments, and reference() takes and returns one part's arrays. A program takes and returns all parts, laid end to end along the dimension named above; an argument that names none is the same for every part. Nothing has to cross between parts.
Inputs may be any that keep to these rules, and one draw needn't show every extreme that they name: `window_tiles`: row i holds 4 different tiles of a frame, and its first entry is i.
All inputs are finite; a program needn't handle non-finite values.
Results may differ from the reference program's by a relative error of at most 0.015.
Values may be sent and summed in bfloat16 or wider, within the bound.
No kernel may reach another device: no remote copies, remote signals or barrier semaphores. Data moves between devices by JAX's collectives and lax.ppermute only.
A program may use at most 64 MiB of HBM per device.

```python
import jax
import jax.numpy as jnp
from jax import lax

D = 3072
HD = 128
HS = 8
S = 512
TILE = 64
WIN = 4
FRAMES = 32
TOKENS = 16384
N_TP = 8


def draw_w_qkv(key, part):
    key = jax.random.fold_in(key, 11)
    first, second, third = jax.random.split(key, 3)
    shape = (D, 2, HS * HD)
    queries = jax.random.normal(first, shape, jnp.float32) * D ** (-0.5)
    values = jax.random.normal(third, shape, jnp.float32) * D ** (-0.5)
    keys = jax.random.normal(second, shape, jnp.float32) * D ** (-0.5)
    return jnp.stack([queries, keys, values], axis=1).astype(jnp.bfloat16)


def draw_window_tiles(key, part):
    key = jax.random.fold_in(key, 5)
    tiles = S // TILE
    raw_scores = jax.random.randint(key, (tiles, tiles), 0, 65536, jnp.int32)
    ranked = raw_scores * tiles + jnp.arange(tiles, dtype=jnp.int32)[None, :]
    ranked = ranked + jnp.eye(tiles, dtype=jnp.int32) * (1 << 24)
    chosen_values, chosen = lax.top_k(ranked, WIN)
    return chosen.astype(jnp.int32)


def block_scale(key, extent, shards, low, high):
    loudness = 1.0
    for dim, parts in shards:
        draws = jax.random.uniform(jax.random.fold_in(jax.random.fold_in(key, 6), dim), (parts,), jnp.float32, low / len(shards), high / len(shards))
        loudness = loudness * jnp.repeat(jnp.exp(draws), extent[dim] // parts).reshape((-1,) + (1,) * (len(extent) - 1 - dim))
    return loudness


def bell_draw(rng, dims, deviation, bound, pieces=(), held_as=jnp.bfloat16):
    level = block_scale(rng, dims, pieces, -0.22, 0.18) if pieces else 1.0
    values = jax.random.normal(rng, dims, jnp.float32) * deviation * level
    return jnp.minimum(jnp.maximum(values, -bound), bound).astype(held_as)


def setup_inputs(seed: int = 0, part: int = 0) -> dict:
    key_list = jax.random.split(jax.random.key(seed), 8)
    own_keys = jax.random.split(jax.random.fold_in(key_list[7], part), 8)
    hidden = bell_draw(own_keys[0], (TOKENS, D), 1.0, 6.0, ((0, 32), (1, 8)))
    shift_mod = bell_draw(own_keys[1], (D,), 0.5, 3.0, (), jnp.float32)
    scale_mod = bell_draw(own_keys[2], (D,), 0.5, 3.0, (), jnp.float32)
    gate = bell_draw(own_keys[3], (D,), 1.0, 4.0, (), jnp.float32)
    w_qkv = draw_w_qkv(jax.random.fold_in(key_list[7], 71), part)
    w_out = bell_draw(key_list[5], (2, HS * HD, D), (2 * HS * HD) ** -0.5, 0.125, ((1, 8),))
    window_tiles = draw_window_tiles(jax.random.fold_in(key_list[7], 71), part)
    return {"hidden": hidden, "shift_mod": shift_mod, "scale_mod": scale_mod, "gate": gate, "w_qkv": w_qkv, "w_out": w_out, "window_tiles": window_tiles}


def layer_normed(hidden, shift_mod, scale_mod):
    source = hidden.astype(jnp.float32)
    middle = lax.optimization_barrier(jnp.mean(source, -1, keepdims=True))
    centred = source - middle
    spread = lax.optimization_barrier(jnp.mean(centred * centred, -1, keepdims=True))
    return (centred * lax.rsqrt(spread + 1e-06) * (1.0 + scale_mod) + shift_mod).astype(jnp.bfloat16)

def spatial_frame(queries, keys, values, window_tiles):
    tiles = S // TILE
    heads = queries.shape[1]
    query_tiles = queries.reshape(tiles, TILE, heads, HD).astype(jnp.float32)
    key_tiles = jnp.take(keys.reshape(tiles, TILE, heads, HD), window_tiles, axis=0).reshape(tiles, WIN * TILE, heads, HD).astype(jnp.float32)
    value_tiles = jnp.take(values.reshape(tiles, TILE, heads, HD), window_tiles, axis=0).reshape(tiles, WIN * TILE, heads, HD).astype(jnp.float32)
    scores = jnp.einsum('nqhd,nkhd->nhqk', query_tiles, key_tiles) * float(HD) ** (-0.5)
    weights = jax.nn.softmax(scores, axis=-1).astype(jnp.bfloat16)
    result = jnp.einsum('nhqk,nkhd->nqhd', weights.astype(jnp.float32), value_tiles)
    return result.astype(jnp.bfloat16).reshape(S, heads * HD)

def reference(hidden, shift_mod, scale_mod, gate, w_qkv, w_out, window_tiles):
    normed = layer_normed(hidden, shift_mod, scale_mod)
    flat_weight = w_qkv.reshape(D, 6 * HS * HD)

    def project(frame_rows):
        return jnp.dot(frame_rows, flat_weight, preferred_element_type=jnp.float32).astype(jnp.bfloat16)
    projected = lax.map(project, normed.reshape(FRAMES, S, D)).reshape(FRAMES, S, 3, 2, HS, HD)

    def spatial_one(frame_block):
        return spatial_frame(frame_block[:, 0, 0], frame_block[:, 1, 0], frame_block[:, 2, 0], window_tiles)
    spatial = lax.map(spatial_one, projected)
    queries = projected[:, :, 0, 1].astype(jnp.float32)
    keys = projected[:, :, 1, 1].astype(jnp.float32)
    values = projected[:, :, 2, 1].astype(jnp.float32)
    scores = jnp.einsum('fphd,gphd->phfg', queries, keys) * float(HD) ** (-0.5)
    weights = jax.nn.softmax(scores, axis=-1).astype(jnp.bfloat16)
    temporal = jnp.einsum('phfg,gphd->fphd', weights.astype(jnp.float32), values).astype(jnp.bfloat16).reshape(FRAMES, S, HS * HD)
    local_heads = HS // N_TP
    attended = jnp.stack([spatial, temporal], axis=2).reshape(TOKENS, 2, N_TP, local_heads * HD)
    grouped = w_out.reshape(2, N_TP, local_heads * HD, D)
    branch = jnp.zeros((TOKENS, D), jnp.float32)
    for group in range(N_TP):
        partial_sum = jnp.dot(attended[:, :, group].reshape(TOKENS, 2 * local_heads * HD), grouped[:, group].reshape(2 * local_heads * HD, D), preferred_element_type=jnp.float32).astype(jnp.bfloat16)
        partial_sum = lax.optimization_barrier(partial_sum)
        branch = branch + partial_sum.astype(jnp.float32)
    return (hidden.astype(jnp.float32) + gate * branch).astype(jnp.bfloat16)
```

```python
import functools

import jax
import jax.numpy as jnp
from jax import lax
from jax.experimental import pallas as pl
from jax.experimental.pallas import tpu as pltpu
from jax.sharding import Mesh, PartitionSpec as P

D = 3072
HD = 128
TILE = 64
WIN = 4
F32 = jnp.float32
BF16 = jnp.bfloat16
VMEM = pl.BlockSpec(memory_space=pltpu.VMEM)
SMEM = pl.BlockSpec(memory_space=pltpu.SMEM)
HBM = pl.BlockSpec(memory_space=pl.ANY)

Y_PLACE = (0, 2, 1, 3)


def along_z(value, step):
    return lax.ppermute(value, "z", [(i, (i + step) % 16) for i in range(16)])


def along_x(value, step):
    return lax.ppermute(value, "x", [(i, (i + step) % 4) for i in range(4)])


def along_y(value, step):
    return lax.ppermute(value, ("yl", "dp"), [(Y_PLACE[i], Y_PLACE[(i + step) % 4]) for i in range(4)])


def other_core(value):
    return lax.ppermute(value, "c", [(0, 1), (1, 0)])


def over_tp(value):
    mine = jnp.stack([value, along_x(value, 1), along_x(value, -1), along_x(value, 2)])
    return mine, other_core(mine)


def normalise(order, mine, theirs, shift, scale, normed):
    def rows_of(step, _):
        rows = pl.ds(pl.multiple_of(step * 16, 16), 16)
        blocks = [mine[j, rows, :].astype(F32) for j in range(4)] + [theirs[j, rows, :].astype(F32) for j in range(4)]
        middle = jnp.sum(sum(blocks), -1, keepdims=True) * (1.0 / D)
        blocks = [block - middle for block in blocks]
        spread = jnp.sum(sum(block * block for block in blocks), -1, keepdims=True) * (1.0 / D)
        inverse = lax.rsqrt(spread + 1e-06)
        for j in range(8):
            group = order[j]
            value = blocks[j] * inverse * (1.0 + scale[pl.ds(group, 1), :]) + shift[pl.ds(group, 1), :]
            normed[rows, pl.ds(pl.multiple_of(group * 384, 128), 384)] = value.astype(BF16)
        return 0

    lax.fori_loop(0, 32, rows_of, 0)


def project(normed, weight, projected):
    def tile_of(step, _):
        rows = pl.ds(pl.multiple_of(step * 128, 128), 128)
        projected[rows, :] = jnp.dot(normed[rows, :], weight[...], preferred_element_type=F32).astype(BF16)
        return 0

    lax.fori_loop(0, 4, tile_of, 0)


def softmax(scores):
    raised = jnp.exp(scores - jnp.max(scores, -1, keepdims=True))
    return (raised / jnp.sum(raised, -1, keepdims=True)).astype(BF16)


def scores_of(queries, keys):
    return lax.dot_general(queries, keys, (((1,), (1,)), ((), ())), preferred_element_type=F32) * float(HD) ** (-0.5)


def temporal_kernel(layout, *refs):
    pieces = refs[: len(layout)]
    order, places, mine, theirs, shift, scale, out, weight, normed, projected, sem = refs[len(layout) :]
    copies = []
    at = 0
    for piece, count in zip(pieces, layout):
        for i in range(count):
            start = pl.multiple_of(places[at] * 96, 32)
            copies.append(pltpu.make_async_copy(piece.at[pl.ds(i * 96, 96), :], weight.at[pl.ds(start, 96), :], sem.at[at]))
            copies[-1].start()
            at += 1
    normalise(order, mine, theirs, shift, scale, normed)
    for copy in copies:
        copy.wait()
    project(normed, weight, projected)

    def tile_of(step, _):
        rows = pl.ds(pl.multiple_of(step * 128, 128), 128)
        scores = scores_of(projected[rows, 0:128], projected[:, 128:256])
        at_row = lax.broadcasted_iota(jnp.int32, scores.shape, 0) % 16
        at_column = lax.broadcasted_iota(jnp.int32, scores.shape, 1) % 16
        weights = softmax(jnp.where(at_row == at_column, scores, -1e30))
        out[rows, :] = jnp.dot(weights, projected[:, 256:384], preferred_element_type=F32).astype(BF16)
        return 0

    lax.fori_loop(0, 4, tile_of, 0)


def spatial_kernel(gathered, order, yl, window, mine, theirs, shift, scale, out, weight, normed, projected, sem):
    copies = []
    for z in range(16):
        for half in range(2):
            start = pl.multiple_of(((yl[0] + half) % 2 * 16 + z) * 96, 32)
            copies.append(
                pltpu.make_async_copy(
                    gathered.at[pl.ds(z * 192 + half * 96, 96), :], weight.at[pl.ds(start, 96), :], sem.at[z * 2 + half]
                )
            )
            copies[-1].start()
    normalise(order, mine, theirs, shift, scale, normed)
    for copy in copies:
        copy.wait()
    project(normed, weight, projected)

    def tile_of(step, _):
        rows = pl.ds(pl.multiple_of(step * TILE, TILE), TILE)
        chosen = [pl.ds(pl.multiple_of(window[step, i] * TILE, TILE), TILE) for i in range(WIN)]
        keys = jnp.concatenate([projected[there, 128:256] for there in chosen], 0)
        values = jnp.concatenate([projected[there, 256:384] for there in chosen], 0)
        weights = softmax(scores_of(projected[rows, 0:128], keys))
        out[rows, :] = jnp.dot(weights, values, preferred_element_type=F32).astype(BF16)
        return 0

    lax.fori_loop(0, 8, tile_of, 0)


def heads_kernel(kind, order, mine, theirs, w_out, *refs):
    wide = refs[-1]
    total = jnp.zeros((512, 384), F32)
    for j in range(8):
        block = mine[j] if j < 4 else theirs[j - 4]
        wide[:, pl.ds(pl.multiple_of(order[j] * HD, HD), HD)] = block
    rows = jnp.concatenate([w_out[g, pl.ds(kind * HD, HD), :] for g in range(8)], 0)
    total = jnp.dot(wide[...], rows, preferred_element_type=F32)
    if kind == 0:
        refs[0][...] = total
    else:
        spatial, hidden, gate, out = refs[:4]
        out[...] = (hidden[...].astype(F32) + gate[...] * (total + spatial[...])).astype(BF16)


def params(flops, size):
    return dict(
        compiler_params=pltpu.CompilerParams(vmem_limit_bytes=32 * 1024 * 1024),
        cost_estimate=pl.CostEstimate(flops=flops, bytes_accessed=size, transcendentals=0),
    )


QKV_SCRATCH = [
    pltpu.VMEM((D, 384), BF16),
    pltpu.VMEM((512, D), BF16),
    pltpu.VMEM((512, 384), BF16),
    pltpu.SemaphoreType.DMA((32,)),
]


def body(hidden, shift_mod, scale_mod, gate, w_qkv, w_out, window_tiles):
    x, core, z, yl = (lax.axis_index(name) for name in ("x", "c", "z", "yl"))
    shift, scale = shift_mod.reshape(8, 384), scale_mod.reshape(8, 384)
    order = jnp.stack([(x + dx) % 4 * 2 + side for side in (core, 1 - core) for dx in (0, 3, 1, 2)]).astype(jnp.int32)

    w_temporal = w_qkv[:, :, 1].reshape(96, 384)
    w_spatial = w_qkv[:, :, 0].reshape(96, 384)

    pair = jnp.concatenate([w_spatial, lax.ppermute(w_spatial, "yl", [(0, 1), (1, 0)])], 0)
    gathered = lax.all_gather(pair, "z", axis=0, tiled=True)

    by_position = lax.all_to_all(
        hidden.reshape(32, 16, 384), ("yl", "z"), split_axis=0, concat_axis=0, tiled=True
    ).reshape(512, 384)

    first = jnp.concatenate([w_temporal, along_z(w_temporal, 5), along_z(w_temporal, -5)], 0)
    below = along_z(first, 1)
    above = along_z(first, -1)
    near_a = along_y(jnp.concatenate([first[:96], below], 0), 1)
    near_b = along_y(jnp.concatenate([first[96:], above], 0), -1)
    far_below = along_z(below, 1)
    far_above = along_z(above, -1)
    opposite = along_z(above[192:], -2)
    near_c = along_y(jnp.concatenate([far_below, opposite], 0), 1)
    near_d = along_y(far_above, -1)
    blocks = (
        (first, (0, -5, 5), 0),
        (below, (-1, -6, 4), 0),
        (above, (1, -4, 6), 0),
        (far_below, (-2, -7, 3), 0),
        (far_above, (2, -3, 7), 0),
        (opposite, (8,), 0),
        (near_a, (0, -1, -6, 4), 1),
        (near_b, (-5, 5, 1, -4, 6), 1),
        (near_c, (-2, -7, 3, 8), 1),
        (near_d, (2, -3, 7), 1),
    )
    places = jnp.stack(
        [(yl + side) % 2 * 16 + (z + offset + 16) % 16 for _, offsets, side in blocks for offset in offsets]
    ).astype(jnp.int32)

    mine, theirs = over_tp(hidden)
    mine_t, theirs_t = over_tp(by_position)

    columns = lax.all_to_all(
        w_out.reshape(256, 8, 384).transpose(1, 0, 2), ("x", "c"), split_axis=0, concat_axis=0, tiled=True
    )

    layout = tuple(len(offsets) for _, offsets, _ in blocks)
    temporal = pl.pallas_call(
        functools.partial(temporal_kernel, layout),
        out_shape=jax.ShapeDtypeStruct((512, HD), BF16),
        in_specs=[HBM] * len(blocks) + [SMEM, SMEM, VMEM, VMEM, VMEM, VMEM],
        out_specs=VMEM,
        scratch_shapes=QKV_SCRATCH,
        name="temporal",
        **params(1_300_000_000, 6_000_000),
    )(*[block for block, _, _ in blocks], order, places, mine_t, theirs_t, shift, scale)
    temporal = lax.all_to_all(
        temporal.reshape(32, 16, HD), ("yl", "z"), split_axis=0, concat_axis=0, tiled=True
    ).reshape(512, HD)

    spatial = pl.pallas_call(
        spatial_kernel,
        out_shape=jax.ShapeDtypeStruct((512, HD), BF16),
        in_specs=[HBM, SMEM, SMEM, SMEM, VMEM, VMEM, VMEM, VMEM],
        out_specs=VMEM,
        scratch_shapes=QKV_SCRATCH,
        name="spatial",
        **params(1_300_000_000, 6_000_000),
    )(gathered, order, yl.astype(jnp.int32).reshape(1), window_tiles, mine, theirs, shift, scale)

    spatial_heads = over_tp(spatial)
    temporal_heads = over_tp(temporal)
    gate_here = lax.dynamic_slice_in_dim(gate, (x * 2 + core) * 384, 384).reshape(1, 384)
    share = pl.pallas_call(
        functools.partial(heads_kernel, 0),
        out_shape=jax.ShapeDtypeStruct((512, 384), F32),
        in_specs=[SMEM, VMEM, VMEM, VMEM],
        out_specs=VMEM,
        scratch_shapes=[pltpu.VMEM((512, 1024), BF16)],
        name="spatial_share",
        **params(400_000_000, 3_000_000),
    )(order, *spatial_heads, columns)
    return pl.pallas_call(
        functools.partial(heads_kernel, 1),
        out_shape=jax.ShapeDtypeStruct((512, 384), BF16),
        in_specs=[SMEM] + [VMEM] * 6,
        out_specs=VMEM,
        scratch_shapes=[pltpu.VMEM((512, 1024), BF16)],
        name="mixed",
        **params(400_000_000, 4_000_000),
    )(order, *temporal_heads, columns, share, hidden, gate_here)


def solution(mesh):
    fine = Mesh(mesh.devices.reshape(2, 16, 4, 2, 2), ("yl", "z", "x", "c", "dp"))
    seq, tp = ("yl", "z"), ("x", "c")
    in_specs = (
        P(("dp",) + seq, tp),
        P("dp"),
        P("dp"),
        P("dp"),
        P(seq, None, None, tp),
        P(None, tp, None),
        P(),
    )
    out_specs = P(("dp",) + seq, tp)
    return jax.shard_map(body, mesh=fine, in_specs=in_specs, out_specs=out_specs, check_vma=False)
```

```python
import functools

import jax
import jax.numpy as jnp
from jax import lax
from jax.experimental import pallas as pl
from jax.experimental.pallas import tpu as pltpu
from jax.sharding import Mesh, PartitionSpec as P

D = 3072
HD = 128
TILE = 64
WIN = 4
F32 = jnp.float32
BF16 = jnp.bfloat16
VMEM = pl.BlockSpec(memory_space=pltpu.VMEM)
SMEM = pl.BlockSpec(memory_space=pltpu.SMEM)
HBM = pl.BlockSpec(memory_space=pl.ANY)
COLUMNS = pl.BlockSpec((8, 256, 384), lambda i: (0, 2, 0))
ROWS = pl.BlockSpec((256, 384), lambda i: (i, 0))
HEADS = pl.BlockSpec((2, 2, 256, HD), lambda i: (0, 0, i, 0))

Y_PLACE = (0, 2, 1, 3)


def along_z(value, step):
    return lax.ppermute(value, ("zh", "zl"), [(i, (i + step) % 16) for i in range(16)])


def along_x(value, step):
    return lax.ppermute(value, "x", [(i, (i + step) % 4) for i in range(4)])


def along_y(value, step):
    return lax.ppermute(value, ("yl", "dp"), [(Y_PLACE[i], Y_PLACE[(i + step) % 4]) for i in range(4)])


def tie(*values):
    return lax.optimization_barrier(values)


def norm_kernel(blocks_ref, shift, scale, normed):
    def rows_of(step, _):
        rows = pl.ds(pl.multiple_of(step * 16, 16), 16)
        blocks = [blocks_ref[j, rows, :].astype(F32) for j in range(8)]
        middle = jnp.sum(sum(blocks), -1, keepdims=True) * (1.0 / D)
        blocks = [block - middle for block in blocks]
        spread = jnp.sum(sum(block * block for block in blocks), -1, keepdims=True) * (1.0 / D)
        inverse = lax.rsqrt(spread + 1e-06)
        for j in range(8):
            value = blocks[j] * inverse * (1.0 + scale[pl.ds(j, 1), :]) + shift[pl.ds(j, 1), :]
            normed[rows, j * 384 : (j + 1) * 384] = value.astype(BF16)
        return 0

    lax.fori_loop(0, normed.shape[0] // 16, rows_of, 0, unroll=4)


def project(normed, weight, total, out):
    for step in range(4):
        part = weight[step * 2 : step * 2 + 2].reshape(768, 384)
        term = jnp.dot(normed[:, step * 768 : step * 768 + 768], part, preferred_element_type=F32)
        if step == 0:
            total[...] = term
        elif step < 3:
            total[...] += term
        else:
            out[...] = (total[...] + term).astype(BF16)


def softmax(scores):
    raised = jnp.exp(scores - jnp.max(scores, -1, keepdims=True))
    return (raised / jnp.sum(raised, -1, keepdims=True)).astype(BF16)


def scores_of(queries, keys):
    return lax.dot_general(queries, keys, (((1,), (1,)), ((), ())), preferred_element_type=F32) * float(HD) ** (-0.5)


def temporal_project_kernel(
    place, own, below, above, far_below, far_above, near_own, near_sides, near_far, normed, out, weight, total, sem
):
    here, there = place[0] * 4, (1 - place[0]) * 4
    pieces = (
        (own, here, 4, 0),
        (below, here, 4, 3),
        (above, here, 4, 1),
        (far_below, here, 2, 2),
        (far_above, here + 2, 2, 2),
        (near_own, there, 4, 0),
        (near_sides.at[0:4], there, 4, 3),
        (near_sides.at[4:8], there, 4, 1),
        (near_far, there, 4, 2),
    )
    copies = [
        pltpu.make_async_copy(piece, weight.at[pl.ds(start, count), (place[1] + ahead) % 4], sem.at[i])
        for i, (piece, start, count, ahead) in enumerate(pieces)
    ]
    for copy in copies:
        copy.start()
    for copy in copies:
        copy.wait()
    project(normed, weight, total, out)


def temporal_kernel(projected, out):
    def tile_of(step, _):
        rows = pl.ds(pl.multiple_of(step * 128, 128), 128)
        scores = scores_of(projected[rows, 0:128], projected[:, 128:256])
        at_row = lax.broadcasted_iota(jnp.int32, scores.shape, 0) % 16
        at_column = lax.broadcasted_iota(jnp.int32, scores.shape, 1) % 16
        weights = softmax(jnp.where(at_row == at_column, scores, -1e30))
        out[rows, :] = jnp.dot(weights, projected[:, 256:384], preferred_element_type=F32).astype(BF16)
        return 0

    lax.fori_loop(0, 4, tile_of, 0)


def spatial_kernel(gathered, place, window, normed, out, weight, total, projected, sem):
    copies = []
    for z in range(16):
        for half in range(2):
            start = (place[0] + half) % 2 * 4 + z // 4
            copies.append(
                pltpu.make_async_copy(gathered.at[z, pl.ds(half * 96, 96)], weight.at[start, z % 4], sem.at[z * 2 + half])
            )
            copies[-1].start()
    for copy in copies:
        copy.wait()
    project(normed, weight, total, projected)

    def tile_of(step, _):
        rows = pl.ds(pl.multiple_of(step * TILE, TILE), TILE)
        chosen = [pl.ds(pl.multiple_of(window[step, i] * TILE, TILE), TILE) for i in range(WIN)]
        keys = jnp.concatenate([projected[there, 128:256] for there in chosen], 0)
        values = jnp.concatenate([projected[there, 256:384] for there in chosen], 0)
        weights = softmax(scores_of(projected[rows, 0:128], keys))
        out[rows, :] = jnp.dot(weights, values, preferred_element_type=F32).astype(BF16)
        return 0

    lax.fori_loop(0, 8, tile_of, 0)


def rows_of_kind(w_out, kind):
    return jnp.concatenate([w_out[g, kind * HD : (kind + 1) * HD, :] for g in range(8)], 0)


def share_kernel(heads, w_out, share):
    wide = jnp.concatenate([heads[g] for g in range(8)], 1)
    share[...] = jnp.dot(wide, rows_of_kind(w_out, 0), preferred_element_type=F32)


def mixed_kernel(low, high, w_out, share, hidden, gate, out):
    wide = jnp.concatenate([(low if x < 2 else high)[side, x % 2] for x in range(4) for side in range(2)], 1)
    total = jnp.dot(wide, rows_of_kind(w_out, 1), preferred_element_type=F32)
    out[...] = (hidden[...].astype(F32) + gate[...] * (total + share[...])).astype(BF16)


def params(flops, size):
    return dict(
        compiler_params=pltpu.CompilerParams(vmem_limit_bytes=56 * 1024 * 1024),
        cost_estimate=pl.CostEstimate(flops=flops, bytes_accessed=size, transcendentals=0),
    )


def body(hidden, shift_mod, scale_mod, gate, w_qkv, w_out, window_tiles):
    x, core, zl, yl = (lax.axis_index(name) for name in ("x", "c", "zl", "yl"))
    place = jnp.stack([yl, zl]).astype(jnp.int32)
    shift, scale = shift_mod.reshape(8, 384), scale_mod.reshape(8, 384)

    w_temporal = w_qkv[:, :, 1].reshape(96, 384)
    w_spatial = w_qkv[:, :, 0].reshape(96, 384)
    hidden_now, w_spatial = tie(hidden, w_spatial)

    pair = jnp.concatenate([w_spatial, lax.ppermute(w_spatial, "yl", [(0, 1), (1, 0)])], 0)
    gathered = lax.all_gather(pair, ("zh", "zl"), axis=0)

    sent = jnp.concatenate(
        [jnp.broadcast_to(hidden_now[None], (8, 512, 384)), w_out.reshape(256, 8, 384).transpose(1, 0, 2)], 1
    )
    arrived = lax.all_to_all(sent, ("x", "c"), split_axis=0, concat_axis=0, tiled=True)

    own = lax.all_gather(w_temporal, "zh", axis=0)
    below, above = along_z(own, 1), along_z(own, -1)
    far_below, far_above = along_z(own[:2], 2), along_z(own[2:], -2)
    near_own = along_y(own, 1)
    near_sides = along_y(jnp.concatenate([below, above], 0), -1)
    near_far = along_y(jnp.concatenate([far_below, far_above], 0), 1)

    normed = pl.pallas_call(
        norm_kernel,
        out_shape=jax.ShapeDtypeStruct((512, D), BF16),
        grid=(8,),
        in_specs=[
            pl.BlockSpec((8, 64, 384), lambda i: (0, i, 0)),
            pl.BlockSpec((8, 384), lambda i: (0, 0)),
            pl.BlockSpec((8, 384), lambda i: (0, 0)),
        ],
        out_specs=pl.BlockSpec((64, D), lambda i: (i, 0)),
        name="norm",
        **params(20_000_000, 6_000_000),
    )(arrived, shift, scale)

    projected = pl.pallas_call(
        temporal_project_kernel,
        out_shape=jax.ShapeDtypeStruct((512, 384), BF16),
        in_specs=[SMEM] + [HBM] * 8 + [VMEM],
        out_specs=VMEM,
        scratch_shapes=[pltpu.VMEM((8, 4, 96, 384), BF16), pltpu.VMEM((512, 384), F32), pltpu.SemaphoreType.DMA((9,))],
        name="temporal_project",
        **params(1_200_000_000, 6_000_000),
    )(place, own, below, above, far_below, far_above, near_own, near_sides, near_far, normed)
    by_position = lax.all_to_all(
        projected.reshape(32, 16, 384), ("yl", "zh", "zl"), split_axis=0, concat_axis=0, tiled=True
    ).reshape(512, 384)

    spatial = pl.pallas_call(
        spatial_kernel,
        out_shape=jax.ShapeDtypeStruct((512, HD), BF16),
        in_specs=[HBM, SMEM, SMEM, VMEM],
        out_specs=VMEM,
        scratch_shapes=[
            pltpu.VMEM((8, 4, 96, 384), BF16),
            pltpu.VMEM((512, 384), F32),
            pltpu.VMEM((512, 384), BF16),
            pltpu.SemaphoreType.DMA((32,)),
        ],
        name="spatial",
        **params(1_300_000_000, 6_000_000),
    )(gathered, place, window_tiles, normed)
    by_position, spatial = tie(by_position, spatial)
    spatial_heads = lax.all_gather(spatial, ("x", "c"), axis=0)

    temporal = pl.pallas_call(
        temporal_kernel,
        out_shape=jax.ShapeDtypeStruct((512, HD), BF16),
        in_specs=[VMEM],
        out_specs=VMEM,
        name="temporal",
        **params(140_000_000, 500_000),
    )(by_position)
    temporal = lax.all_to_all(
        temporal.reshape(32, 16, HD), ("yl", "zh", "zl"), split_axis=0, concat_axis=0, tiled=True
    ).reshape(512, HD)
    line = lax.all_gather(temporal, "x", axis=0)
    low, high = lax.all_gather(line[:2], "c", axis=0), lax.all_gather(line[2:], "c", axis=0)
    gate_here = lax.dynamic_slice_in_dim(gate, (x * 2 + core) * 384, 384).reshape(1, 384)
    share = pl.pallas_call(
        share_kernel,
        out_shape=jax.ShapeDtypeStruct((512, 384), F32),
        grid=(2,),
        in_specs=[pl.BlockSpec((8, 256, HD), lambda i: (0, i, 0)), COLUMNS],
        out_specs=ROWS,
        name="spatial_share",
        **params(400_000_000, 3_000_000),
    )(spatial_heads, arrived)
    return pl.pallas_call(
        mixed_kernel,
        out_shape=jax.ShapeDtypeStruct((512, 384), BF16),
        grid=(2,),
        in_specs=[HEADS, HEADS, COLUMNS, ROWS, ROWS, pl.BlockSpec((1, 384), lambda i: (0, 0))],
        out_specs=ROWS,
        name="mixed",
        **params(400_000_000, 4_000_000),
    )(low, high, arrived, share, hidden, gate_here)


def solution(mesh):
    fine = Mesh(mesh.devices.reshape(2, 4, 4, 4, 2, 2), ("yl", "zh", "zl", "x", "c", "dp"))
    seq, tp = ("yl", "zh", "zl"), ("x", "c")
    in_specs = (
        P(("dp",) + seq, tp),
        P("dp"),
        P("dp"),
        P("dp"),
        P(seq, None, None, tp),
        P(None, tp, None),
        P(),
    )
    out_specs = P(("dp",) + seq, tp)
    return jax.shard_map(body, mesh=fine, in_specs=in_specs, out_specs=out_specs, check_vma=False)
```

```python
import functools

import jax
import jax.numpy as jnp
from jax import lax
from jax.experimental import pallas as pl
from jax.experimental.pallas import tpu as pltpu
from jax.sharding import Mesh, PartitionSpec as P

D = 3072
HD = 128
TILE = 64
WIN = 4
F32 = jnp.float32
BF16 = jnp.bfloat16
VMEM = pl.BlockSpec(memory_space=pltpu.VMEM)
SMEM = pl.BlockSpec(memory_space=pltpu.SMEM)
HBM = pl.BlockSpec(memory_space=pl.ANY)
COLUMNS = pl.BlockSpec((8, 256, 384), lambda i: (0, 2, 0))
ROWS = pl.BlockSpec((256, 384), lambda i: (i, 0))
HEADS = pl.BlockSpec((4, 2, 256, HD), lambda i: (0, 0, i, 0))

Y_PLACE = (0, 2, 1, 3)


def along_z(value, step):
    return lax.ppermute(value, ("zh", "zl"), [(i, (i + step) % 16) for i in range(16)])


def along_x(value, step):
    return lax.ppermute(value, "x", [(i, (i + step) % 4) for i in range(4)])


def along_y(value, step):
    return lax.ppermute(value, ("yl", "dp"), [(Y_PLACE[i], Y_PLACE[(i + step) % 4]) for i in range(4)])


def other_core(value):
    return lax.ppermute(value, "c", [(0, 1), (1, 0)])


def tie(*values):
    return lax.optimization_barrier(values)


def norm_kernel(blocks_ref, shift, scale, normed):
    def rows_of(step, _):
        rows = pl.ds(pl.multiple_of(step * 16, 16), 16)
        blocks = [blocks_ref[j, rows, :].astype(F32) for j in range(8)]
        middle = jnp.sum(sum(blocks), -1, keepdims=True) * (1.0 / D)
        blocks = [block - middle for block in blocks]
        spread = jnp.sum(sum(block * block for block in blocks), -1, keepdims=True) * (1.0 / D)
        inverse = lax.rsqrt(spread + 1e-06)
        for j in range(8):
            value = blocks[j] * inverse * (1.0 + scale[pl.ds(j, 1), :]) + shift[pl.ds(j, 1), :]
            normed[rows, j * 384 : (j + 1) * 384] = value.astype(BF16)
        return 0

    lax.fori_loop(0, normed.shape[0] // 16, rows_of, 0, unroll=4)


def project(normed, weight, parts, sems, fetched):
    copies = [pltpu.make_async_copy(normed.at[:, pl.ds(i * 768, 768)], parts.at[i], sems.at[i]) for i in range(4)]
    for copy in copies:
        copy.start()
    for copy in fetched:
        copy.wait()
    total = 0.0
    for i, copy in enumerate(copies):
        copy.wait()
        rows = weight[i * 2 : i * 2 + 2].reshape(768, 384)
        total += jnp.dot(parts[i], rows, preferred_element_type=F32)
    return total.astype(BF16)


def softmax(scores):
    raised = jnp.exp(scores - jnp.max(scores, -1, keepdims=True))
    return (raised * (1.0 / jnp.sum(raised, -1, keepdims=True))).astype(BF16)


def scores_of(queries, keys):
    return lax.dot_general(queries, keys, (((1,), (1,)), ((), ())), preferred_element_type=F32) * float(HD) ** (-0.5)


def sent_kernel(hidden, w_out, sent, sem):
    copies = []
    for g in range(8):
        copies.append(pltpu.make_async_copy(hidden, sent.at[g, pl.ds(0, 512)], sem.at[len(copies)]))
        for kind in range(2):
            columns = w_out.at[kind, :, pl.ds(g * 384, 384)]
            copies.append(
                pltpu.make_async_copy(columns, sent.at[g, pl.ds(512 + kind * HD, HD)], sem.at[len(copies)])
            )
    for copy in copies:
        copy.start()
    for copy in copies:
        copy.wait()


def fetch(kind, place, pieces, weight, sem):
    own, below, above, far_below, far_above, near_own, near_low, near_high = pieces
    own, below, above, far_below, far_above, near_own = (
        piece.at[:, pl.ds(kind * 96, 96)] for piece in (own, below, above, far_below, far_above, near_own)
    )
    here, there = place[0] * 4, (1 - place[0]) * 4
    parts = (
        (own, here, 4, 0),
        (below, here, 4, 3),
        (above, here, 4, 1),
        (far_below, here, 2, 2),
        (far_above, here + 2, 2, 2),
        (near_own, there, 4, 0),
        (near_low.at[0:4], there, 4, 3),
        (near_low.at[4:6], there, 2, 2),
        (near_high.at[0:4], there, 4, 1),
        (near_high.at[4:6], there + 2, 2, 2),
    )
    copies = [
        pltpu.make_async_copy(part, weight.at[pl.ds(start, count), (place[1] + ahead) % 4], sem.at[i])
        for i, (part, start, count, ahead) in enumerate(parts)
    ]
    for copy in copies:
        copy.start()
    return copies


def temporal_project_kernel(place, *refs):
    normed, out, weight, parts, sem, sems = refs[8:]
    out[...] = project(normed, weight, parts, sems, fetch(1, place, refs[:8], weight, sem))


def temporal_kernel(projected, out):
    keys, values = projected[:, 128:256], projected[:, 256:384]
    at_row = lax.broadcasted_iota(jnp.int32, (128, 512), 0) % 16
    at_column = lax.broadcasted_iota(jnp.int32, (128, 512), 1) % 16
    for step in range(4):
        rows = slice(step * 128, step * 128 + 128)
        scores = scores_of(projected[rows, 0:128], keys)
        weights = softmax(jnp.where(at_row == at_column, scores, -1e30))
        out[rows, :] = jnp.dot(weights, values, preferred_element_type=F32).astype(BF16)


def spatial_kernel(place, *refs):
    window, normed, out, weight, parts, projected, sem, sems = refs[8:]
    projected[...] = project(normed, weight, parts, sems, fetch(0, place, refs[:8], weight, sem))

    def tile_of(step, _):
        rows = pl.ds(pl.multiple_of(step * TILE, TILE), TILE)
        chosen = [pl.ds(pl.multiple_of(window[step, i] * TILE, TILE), TILE) for i in range(WIN)]
        keys = jnp.concatenate([projected[there, 128:256] for there in chosen], 0)
        values = jnp.concatenate([projected[there, 256:384] for there in chosen], 0)
        weights = softmax(scores_of(projected[rows, 0:128], keys))
        out[rows, :] = jnp.dot(weights, values, preferred_element_type=F32).astype(BF16)
        return 0

    lax.fori_loop(0, 8, tile_of, 0, unroll=True)


def mixed_kernel(core, mine, theirs, w_out, hidden, gate, out, wide):
    for side, heads in ((core[0], mine), (1 - core[0], theirs)):
        for j, ahead in enumerate((0, 3, 1, 2)):
            group = (core[1] + ahead) % 4 * 2 + side
            for kind in range(2):
                wide[:, pl.ds(pl.multiple_of(group * 256 + kind * HD, HD), HD)] = heads[j, kind]
    total = jnp.dot(wide[...], w_out[...].reshape(2048, 384), preferred_element_type=F32)
    out[...] = (hidden[...].astype(F32) + gate[...] * total).astype(BF16)


def params(flops, size):
    return dict(
        compiler_params=pltpu.CompilerParams(vmem_limit_bytes=56 * 1024 * 1024),
        cost_estimate=pl.CostEstimate(flops=flops, bytes_accessed=size, transcendentals=0),
    )


def body(hidden, shift_mod, scale_mod, gate, w_qkv, w_out, window_tiles):
    x, core, zl, yl = (lax.axis_index(name) for name in ("x", "c", "zl", "yl"))
    place = jnp.stack([yl, zl]).astype(jnp.int32)
    shift, scale = shift_mod.reshape(8, 384), scale_mod.reshape(8, 384)

    shards = jnp.concatenate([w_qkv[:, :, 0].reshape(96, 384), w_qkv[:, :, 1].reshape(96, 384)], 0)

    sent = pl.pallas_call(
        sent_kernel,
        out_shape=jax.ShapeDtypeStruct((8, 768, 384), BF16),
        in_specs=[VMEM, VMEM],
        out_specs=HBM,
        scratch_shapes=[pltpu.SemaphoreType.DMA((24,))],
        name="sent",
        **params(0, 7_000_000),
    )(hidden, w_out)
    arrived = lax.all_to_all(sent, ("x", "c"), split_axis=0, concat_axis=0, tiled=True)

    own = lax.all_gather(shards, "zh", axis=0)
    below, above = along_z(own, 1), along_z(own, -1)
    far_below, far_above = along_z(own[:2], 2), along_z(own[2:], -2)
    near_own = along_y(own, 1)
    weights = tie(own, below, above, far_below, far_above, near_own)

    def near(kind, own, below, above, far_below, far_above, near_own):
        rows = slice(kind * 96, kind * 96 + 96)
        low = along_y(jnp.concatenate([below[:, rows], far_below[:, rows]], 0), 1)
        return low, along_y(jnp.concatenate([above[:, rows], far_above[:, rows]], 0), -1)

    temporal_weights = tuple(weights) + near(1, *weights)

    normed = pl.pallas_call(
        norm_kernel,
        out_shape=jax.ShapeDtypeStruct((512, D), BF16),
        grid=(4,),
        in_specs=[
            pl.BlockSpec((8, 128, 384), lambda i: (0, i, 0)),
            pl.BlockSpec((8, 384), lambda i: (0, 0)),
            pl.BlockSpec((8, 384), lambda i: (0, 0)),
        ],
        out_specs=pl.BlockSpec((128, D), lambda i: (i, 0)),
        name="norm",
        **params(20_000_000, 6_000_000),
    )(arrived, shift, scale)

    projected = pl.pallas_call(
        temporal_project_kernel,
        out_shape=jax.ShapeDtypeStruct((512, 384), BF16),
        in_specs=[SMEM] + [HBM] * 9,
        out_specs=VMEM,
        scratch_shapes=[
            pltpu.VMEM((8, 4, 96, 384), BF16),
            pltpu.VMEM((4, 512, 768), BF16),
            pltpu.SemaphoreType.DMA((10,)),
            pltpu.SemaphoreType.DMA((4,)),
        ],
        name="temporal_project",
        **params(1_200_000_000, 6_000_000),
    )(place, *temporal_weights, normed)
    by_position = lax.all_to_all(
        projected.reshape(32, 16, 384), ("yl", "zh", "zl"), split_axis=0, concat_axis=0, tiled=True
    ).reshape(512, 384)

    *weights, _ = tie(*weights, projected)
    by_position, *near_spatial = tie(by_position, *near(0, *weights))
    spatial_weights = tuple(weights) + tuple(near_spatial)

    temporal = pl.pallas_call(
        temporal_kernel,
        out_shape=jax.ShapeDtypeStruct((512, HD), BF16),
        in_specs=[VMEM],
        out_specs=VMEM,
        name="temporal",
        **params(140_000_000, 500_000),
    )(by_position)
    temporal = lax.all_to_all(
        temporal.reshape(32, 16, HD), ("yl", "zh", "zl"), split_axis=0, concat_axis=0, tiled=True
    ).reshape(512, HD)
    spatial = pl.pallas_call(
        spatial_kernel,
        out_shape=jax.ShapeDtypeStruct((512, HD), BF16),
        in_specs=[SMEM] + [HBM] * 8 + [SMEM, HBM],
        out_specs=VMEM,
        scratch_shapes=[
            pltpu.VMEM((8, 4, 96, 384), BF16),
            pltpu.VMEM((4, 512, 768), BF16),
            pltpu.VMEM((512, 384), BF16),
            pltpu.SemaphoreType.DMA((10,)),
            pltpu.SemaphoreType.DMA((4,)),
        ],
        name="spatial",
        **params(1_300_000_000, 6_000_000),
    )(place, *spatial_weights, window_tiles, normed)

    heads = jnp.stack([spatial, temporal])
    mine = jnp.stack([heads, along_x(heads, 1), along_x(heads, -1), along_x(heads, 2)])
    theirs = other_core(mine)
    gate_here = lax.dynamic_slice_in_dim(gate, (x * 2 + core) * 384, 384).reshape(1, 384)
    return pl.pallas_call(
        mixed_kernel,
        out_shape=jax.ShapeDtypeStruct((512, 384), BF16),
        grid=(2,),
        in_specs=[SMEM, HEADS, HEADS, COLUMNS, ROWS, pl.BlockSpec((1, 384), lambda i: (0, 0))],
        out_specs=ROWS,
        scratch_shapes=[pltpu.VMEM((256, 2048), BF16)],
        name="mixed",
        **params(800_000_000, 5_000_000),
    )(jnp.stack([core, x]).astype(jnp.int32), mine, theirs, arrived, hidden, gate_here)


def solution(mesh):
    fine = Mesh(mesh.devices.reshape(2, 4, 4, 4, 2, 2), ("yl", "zh", "zl", "x", "c", "dp"))
    seq, tp = ("yl", "zh", "zl"), ("x", "c")
    in_specs = (
        P(("dp",) + seq, tp),
        P("dp"),
        P("dp"),
        P("dp"),
        P(seq, None, None, tp),
        P(None, tp, None),
        P(),
    )
    out_specs = P(("dp",) + seq, tp)
    return jax.shard_map(body, mesh=fine, in_specs=in_specs, out_specs=out_specs, check_vma=False)
```

```python
import functools

import jax
import jax.numpy as jnp
from jax import lax
from jax.experimental import pallas as pl
from jax.experimental.pallas import tpu as pltpu
from jax.sharding import Mesh, PartitionSpec as P

D = 3072
HD = 128
TILE = 64
WIN = 4
F32 = jnp.float32
BF16 = jnp.bfloat16
VMEM = pl.BlockSpec(memory_space=pltpu.VMEM)
SMEM = pl.BlockSpec(memory_space=pltpu.SMEM)
HBM = pl.BlockSpec(memory_space=pl.ANY)
COLUMNS = pl.BlockSpec((8, 256, 384), lambda i: (0, 2, 0))
ROWS = pl.BlockSpec((256, 384), lambda i: (i, 0))
HEADS = pl.BlockSpec((4, 2, 256, HD), lambda i: (0, 0, i, 0))

Y_PLACE = (0, 2, 1, 3)


def along_z(value, step):
    return lax.ppermute(value, ("zh", "zl"), [(i, (i + step) % 16) for i in range(16)])


def along_x(value, step):
    return lax.ppermute(value, "x", [(i, (i + step) % 4) for i in range(4)])


def along_y(value, step):
    return lax.ppermute(value, ("yl", "dp"), [(Y_PLACE[i], Y_PLACE[(i + step) % 4]) for i in range(4)])


def other_core(value):
    return lax.ppermute(value, "c", [(0, 1), (1, 0)])


def tie(*values):
    return lax.optimization_barrier(values)


def norm_kernel(blocks_ref, shift, scale, normed):
    def rows_of(step, _):
        rows = pl.ds(pl.multiple_of(step * 16, 16), 16)
        blocks = [blocks_ref[j, rows, :].astype(F32) for j in range(8)]
        middle = jnp.sum(sum(blocks), -1, keepdims=True) * (1.0 / D)
        blocks = [block - middle for block in blocks]
        spread = jnp.sum(sum(block * block for block in blocks), -1, keepdims=True) * (1.0 / D)
        inverse = lax.rsqrt(spread + 1e-06)
        for j in range(24):
            block = blocks[j // 3][:, j % 3 * 128 : j % 3 * 128 + 128]
            value = block * inverse * (1.0 + scale[j : j + 1, :]) + shift[j : j + 1, :]
            normed[rows, j * 128 : j * 128 + 128] = value.astype(BF16)
        return 0

    lax.fori_loop(0, normed.shape[0] // 16, rows_of, 0, unroll=4)


def project(normed, weight, parts, sems, fetched):
    copies = [pltpu.make_async_copy(normed.at[:, pl.ds(i * 768, 768)], parts.at[i], sems.at[i]) for i in range(4)]
    for copy in copies:
        copy.start()
    for copy in fetched:
        copy.wait()
    total = 0.0
    for i, copy in enumerate(copies):
        copy.wait()
        rows = weight[i * 2 : i * 2 + 2].reshape(768, 384)
        total += jnp.dot(parts[i], rows, preferred_element_type=F32)
    return total.astype(BF16)


def softmax(scores):
    raised = jnp.exp(scores - jnp.max(scores, -1, keepdims=True))
    return (raised * (1.0 / jnp.sum(raised, -1, keepdims=True))).astype(BF16)


def scores_of(queries, keys):
    return lax.dot_general(queries, keys, (((1,), (1,)), ((), ())), preferred_element_type=F32) * float(HD) ** (-0.5)


def sent_kernel(hidden, w_out, sent, sem):
    copies = []
    for g in range(8):
        copies.append(pltpu.make_async_copy(hidden, sent.at[g, pl.ds(0, 512)], sem.at[len(copies)]))
        for kind in range(2):
            columns = w_out.at[kind, :, pl.ds(g * 384, 384)]
            copies.append(
                pltpu.make_async_copy(columns, sent.at[g, pl.ds(512 + kind * HD, HD)], sem.at[len(copies)])
            )
    for copy in copies:
        copy.start()
    for copy in copies:
        copy.wait()


def fetch(kind, place, pieces, weight, sem):
    own, below, above, far_below, far_above, near_own, near_low, near_high = pieces
    own, below, above, far_below, far_above, near_own = (
        piece.at[:, pl.ds(kind * 96, 96)] for piece in (own, below, above, far_below, far_above, near_own)
    )
    here, there = place[0] * 4, (1 - place[0]) * 4
    parts = (
        (own, here, 4, 0),
        (below, here, 4, 3),
        (above, here, 4, 1),
        (far_below, here, 2, 2),
        (far_above, here + 2, 2, 2),
        (near_own, there, 4, 0),
        (near_low.at[0:4], there, 4, 3),
        (near_low.at[4:6], there, 2, 2),
        (near_high.at[0:4], there, 4, 1),
        (near_high.at[4:6], there + 2, 2, 2),
    )
    copies = [
        pltpu.make_async_copy(part, weight.at[pl.ds(start, count), (place[1] + ahead) % 4], sem.at[i])
        for i, (part, start, count, ahead) in enumerate(parts)
    ]
    for copy in copies:
        copy.start()
    return copies


def temporal_project_kernel(place, *refs):
    normed, out, weight, parts, sem, sems = refs[8:]
    out[...] = project(normed, weight, parts, sems, fetch(1, place, refs[:8], weight, sem))


def temporal_kernel(projected, out):
    keys, values = projected[:, 128:256], projected[:, 256:384]
    at_row = lax.broadcasted_iota(jnp.int32, (128, 512), 0) % 16
    at_column = lax.broadcasted_iota(jnp.int32, (128, 512), 1) % 16
    for step in range(4):
        rows = slice(step * 128, step * 128 + 128)
        scores = scores_of(projected[rows, 0:128], keys)
        weights = softmax(jnp.where(at_row == at_column, scores, -1e30))
        out[rows, :] = jnp.dot(weights, values, preferred_element_type=F32).astype(BF16)


def spatial_kernel(place, *refs):
    window, normed, out, weight, parts, projected, sem, sems = refs[8:]
    projected[...] = project(normed, weight, parts, sems, fetch(0, place, refs[:8], weight, sem))

    def tile_of(step, _):
        rows = pl.ds(pl.multiple_of(step * TILE, TILE), TILE)
        chosen = [pl.ds(pl.multiple_of(window[step, i] * TILE, TILE), TILE) for i in range(WIN)]
        keys = jnp.concatenate([projected[there, 128:256] for there in chosen], 0)
        values = jnp.concatenate([projected[there, 256:384] for there in chosen], 0)
        weights = softmax(scores_of(projected[rows, 0:128], keys))
        out[rows, :] = jnp.dot(weights, values, preferred_element_type=F32).astype(BF16)
        return 0

    lax.fori_loop(0, 8, tile_of, 0, unroll=True)


def heads_times(heads, w_out, wide, x, side):
    for j, ahead in enumerate((0, 3, 1, 2)):
        for kind in range(2):
            wide[:, (j * 2 + kind) * HD : (j * 2 + kind + 1) * HD] = heads[j, kind]
    rows = jnp.concatenate([w_out[(x + ahead) % 4 * 2 + side] for ahead in (0, 3, 1, 2)], 0)
    return jnp.dot(wide[...], rows, preferred_element_type=F32)


def share_kernel(place, heads, w_out, share, wide):
    share[...] = heads_times(heads, w_out, wide, place[2], place[3])


def mixed_kernel(place, heads, w_out, share, hidden, gate, out, wide):
    total = share[...] + heads_times(heads, w_out, wide, place[2], 1 - place[3])
    for k in range(3):
        columns = slice(k * 128, k * 128 + 128)
        scale = gate[pl.ds((place[2] * 2 + place[3]) * 3 + k, 1), :]
        out[:, columns] = (hidden[:, columns].astype(F32) + scale * total[:, columns]).astype(BF16)


def params(flops, size, limit=56):
    return dict(
        compiler_params=pltpu.CompilerParams(vmem_limit_bytes=limit * 1024 * 1024),
        cost_estimate=pl.CostEstimate(flops=flops, bytes_accessed=size, transcendentals=0),
    )


def body(hidden, shift_mod, scale_mod, gate, w_qkv, w_out, window_tiles):
    x, core, zl, yl = (lax.axis_index(name) for name in ("x", "c", "zl", "yl"))
    place = jnp.stack([yl, zl, x, core]).astype(jnp.int32)
    shift, scale, gate = (value.reshape(24, 128) for value in (shift_mod, scale_mod, gate))

    shards = jnp.concatenate([w_qkv[:, :, 0].reshape(96, 384), w_qkv[:, :, 1].reshape(96, 384)], 0)

    sent = pl.pallas_call(
        sent_kernel,
        out_shape=jax.ShapeDtypeStruct((8, 768, 384), BF16),
        in_specs=[VMEM, VMEM],
        out_specs=HBM,
        scratch_shapes=[pltpu.SemaphoreType.DMA((24,))],
        name="sent",
        **params(0, 7_000_000),
    )(hidden, w_out)
    arrived = lax.all_to_all(sent, ("x", "c"), split_axis=0, concat_axis=0, tiled=True)

    own = lax.all_gather(shards, "zh", axis=0)
    below, above = along_z(own, 1), along_z(own, -1)
    far_below, far_above = along_z(own[:2], 2), along_z(own[2:], -2)
    near_own = along_y(own, 1)
    place, window_tiles, *weights = tie(place, window_tiles, own, below, above, far_below, far_above, near_own)

    def near(kind, own, below, above, far_below, far_above, near_own):
        rows = slice(kind * 96, kind * 96 + 96)
        low = along_y(jnp.concatenate([below[:, rows], far_below[:, rows]], 0), 1)
        return low, along_y(jnp.concatenate([above[:, rows], far_above[:, rows]], 0), -1)

    temporal_weights = tuple(weights) + near(1, *weights)

    normed = pl.pallas_call(
        norm_kernel,
        out_shape=jax.ShapeDtypeStruct((512, D), BF16),
        grid=(4,),
        in_specs=[
            pl.BlockSpec((8, 128, 384), lambda i: (0, i, 0)),
            pl.BlockSpec((24, 128), lambda i: (0, 0)),
            pl.BlockSpec((24, 128), lambda i: (0, 0)),
        ],
        out_specs=pl.BlockSpec((128, D), lambda i: (i, 0)),
        name="norm",
        **params(20_000_000, 6_000_000),
    )(arrived, shift, scale)

    projected = pl.pallas_call(
        temporal_project_kernel,
        out_shape=jax.ShapeDtypeStruct((512, 384), BF16),
        in_specs=[SMEM] + [HBM] * 9,
        out_specs=VMEM,
        scratch_shapes=[
            pltpu.VMEM((8, 4, 96, 384), BF16),
            pltpu.VMEM((4, 512, 768), BF16),
            pltpu.SemaphoreType.DMA((10,)),
            pltpu.SemaphoreType.DMA((4,)),
        ],
        name="temporal_project",
        **params(1_200_000_000, 6_000_000),
    )(place, *temporal_weights, normed)
    by_position = lax.all_to_all(
        projected.reshape(32, 16, 384), ("yl", "zh", "zl"), split_axis=0, concat_axis=0, tiled=True
    ).reshape(512, 384)

    *weights, _ = tie(*weights, projected)
    by_position, *near_spatial = tie(by_position, *near(0, *weights))
    spatial_weights = tuple(weights) + tuple(near_spatial)

    temporal = pl.pallas_call(
        temporal_kernel,
        out_shape=jax.ShapeDtypeStruct((512, HD), BF16),
        in_specs=[VMEM],
        out_specs=VMEM,
        name="temporal",
        **params(140_000_000, 500_000),
    )(by_position)
    temporal = lax.all_to_all(
        temporal.reshape(32, 16, HD), ("yl", "zh", "zl"), split_axis=0, concat_axis=0, tiled=True
    ).reshape(512, HD)
    spatial = pl.pallas_call(
        spatial_kernel,
        out_shape=jax.ShapeDtypeStruct((512, HD), BF16),
        in_specs=[SMEM] + [HBM] * 8 + [SMEM, HBM],
        out_specs=VMEM,
        scratch_shapes=[
            pltpu.VMEM((8, 4, 96, 384), BF16),
            pltpu.VMEM((4, 512, 768), BF16),
            pltpu.VMEM((512, 384), BF16),
            pltpu.SemaphoreType.DMA((10,)),
            pltpu.SemaphoreType.DMA((4,)),
        ],
        name="spatial",
        **params(1_300_000_000, 6_000_000),
    )(place, *spatial_weights, window_tiles, normed)

    heads = jnp.stack([spatial, temporal])
    mine = jnp.stack([heads, along_x(heads, 1), along_x(heads, -1), along_x(heads, 2)])
    theirs = other_core(mine)
    share = pl.pallas_call(
        share_kernel,
        out_shape=jax.ShapeDtypeStruct((512, 384), F32),
        grid=(2,),
        in_specs=[SMEM, HEADS, COLUMNS],
        out_specs=ROWS,
        scratch_shapes=[pltpu.VMEM((256, 1024), BF16)],
        name="share",
        **params(400_000_000, 4_000_000, 24),
    )(place, mine, arrived)
    return pl.pallas_call(
        mixed_kernel,
        out_shape=jax.ShapeDtypeStruct((512, 384), BF16),
        grid=(2,),
        in_specs=[SMEM, HEADS, COLUMNS, ROWS, ROWS, pl.BlockSpec((24, 128), lambda i: (0, 0))],
        out_specs=ROWS,
        scratch_shapes=[pltpu.VMEM((256, 1024), BF16)],
        name="mixed",
        **params(400_000_000, 5_000_000, 24),
    )(place, theirs, arrived, share, hidden, gate)


def solution(mesh):
    fine = Mesh(mesh.devices.reshape(2, 4, 4, 4, 2, 2), ("yl", "zh", "zl", "x", "c", "dp"))
    seq, tp = ("yl", "zh", "zl"), ("x", "c")
    in_specs = (
        P(("dp",) + seq, tp),
        P("dp"),
        P("dp"),
        P("dp"),
        P(seq, None, None, tp),
        P(None, tp, None),
        P(),
    )
    out_specs = P(("dp",) + seq, tp)
    return jax.shard_map(body, mesh=fine, in_specs=in_specs, out_specs=out_specs, check_vma=False)
```

```python
import functools

import jax
import jax.numpy as jnp
from jax import lax
from jax.experimental import pallas as pl
from jax.experimental.pallas import tpu as pltpu
from jax.sharding import Mesh, PartitionSpec as P

D = 3072
HD = 128
TILE = 64
WIN = 4
F32 = jnp.float32
BF16 = jnp.bfloat16
VMEM = pl.BlockSpec(memory_space=pltpu.VMEM)
SMEM = pl.BlockSpec(memory_space=pltpu.SMEM)
HBM = pl.BlockSpec(memory_space=pl.ANY)
COLUMNS = pl.BlockSpec((8, 256, 384), lambda i: (0, 2, 0))
ROWS = pl.BlockSpec((256, 384), lambda i: (i, 0))
HEADS = pl.BlockSpec((4, 2, 256, HD), lambda i: (0, 0, i, 0))

Y_PLACE = (0, 2, 1, 3)


def along_z(value, step):
    return lax.ppermute(value, ("zh", "zl"), [(i, (i + step) % 16) for i in range(16)])


def along_x(value, step):
    return lax.ppermute(value, "x", [(i, (i + step) % 4) for i in range(4)])


def along_y(value, step):
    return lax.ppermute(value, ("yl", "dp"), [(Y_PLACE[i], Y_PLACE[(i + step) % 4]) for i in range(4)])


def other_core(value):
    return lax.ppermute(value, "c", [(0, 1), (1, 0)])


def tie(*values):
    return lax.optimization_barrier(values)


def norm_kernel(blocks_ref, shift, scale, normed):
    def rows_of(step, _):
        rows = pl.ds(pl.multiple_of(step * 16, 16), 16)
        blocks = [blocks_ref[j, rows, :].astype(F32) for j in range(8)]
        middle = jnp.sum(sum(blocks), -1, keepdims=True) * (1.0 / D)
        blocks = [block - middle for block in blocks]
        spread = jnp.sum(sum(block * block for block in blocks), -1, keepdims=True) * (1.0 / D)
        inverse = lax.rsqrt(spread + 1e-06)
        for j in range(24):
            block = blocks[j // 3][:, j % 3 * 128 : j % 3 * 128 + 128]
            value = block * inverse * (1.0 + scale[j : j + 1, :]) + shift[j : j + 1, :]
            normed[rows, j * 128 : j * 128 + 128] = value.astype(BF16)
        return 0

    lax.fori_loop(0, normed.shape[0] // 16, rows_of, 0, unroll=4)


def project(normed, weight, parts, sems, fetched):
    copies = [pltpu.make_async_copy(normed.at[:, pl.ds(i * 768, 768)], parts.at[i], sems.at[i]) for i in range(4)]
    for copy in copies:
        copy.start()
    for copy in fetched:
        copy.wait()
    total = 0.0
    for i, copy in enumerate(copies):
        copy.wait()
        rows = weight[i * 2 : i * 2 + 2].reshape(768, 384)
        total += jnp.dot(parts[i], rows, preferred_element_type=F32)
    return total.astype(BF16)


def softmax(scores):
    raised = jnp.exp(scores - jnp.max(scores, -1, keepdims=True))
    return (raised * (1.0 / jnp.sum(raised, -1, keepdims=True))).astype(BF16)


def scores_of(queries, keys):
    return lax.dot_general(queries, keys, (((1,), (1,)), ((), ())), preferred_element_type=F32) * float(HD) ** (-0.5)


def sent_kernel(hidden, w_out, sent, sem):
    copies = []
    for g in range(8):
        copies.append(pltpu.make_async_copy(hidden, sent.at[g, pl.ds(0, 512)], sem.at[len(copies)]))
        for kind in range(2):
            columns = w_out.at[kind, :, pl.ds(g * 384, 384)]
            copies.append(
                pltpu.make_async_copy(columns, sent.at[g, pl.ds(512 + kind * HD, HD)], sem.at[len(copies)])
            )
    for copy in copies:
        copy.start()
    for copy in copies:
        copy.wait()


def fetch(kind, place, pieces, weight, sem):
    own, below, above, far_first, far_second, near_own, near_low, near_high = pieces
    own, below, above, near_own = (piece.at[:, pl.ds(kind * 96, 96)] for piece in (own, below, above, near_own))
    here, there = place[0] * 4, (1 - place[0]) * 4
    parts = (
        (own, here, 4, 0),
        (below, here, 4, 3),
        (above, here, 4, 1),
        (far_first, here, 2, 2),
        (far_second, here + 2, 2, 2),
        (near_own, there, 4, 0),
        (near_low.at[0:4], there, 4, 3),
        (near_low.at[4:6], there + 2, 2, 2),
        (near_high.at[0:4], there, 4, 1),
        (near_high.at[4:6], there, 2, 2),
    )
    copies = [
        pltpu.make_async_copy(part, weight.at[pl.ds(start, count), (place[1] + ahead) % 4], sem.at[i])
        for i, (part, start, count, ahead) in enumerate(parts)
    ]
    for copy in copies:
        copy.start()
    return copies


def temporal_project_kernel(place, *refs):
    normed, out, weight, parts, sem, sems = refs[8:]
    out[...] = project(normed, weight, parts, sems, fetch(1, place, refs[:8], weight, sem))


def temporal_kernel(projected, out):
    keys, values = projected[:, 128:256], projected[:, 256:384]
    at_row = lax.broadcasted_iota(jnp.int32, (128, 512), 0) % 16
    at_column = lax.broadcasted_iota(jnp.int32, (128, 512), 1) % 16
    for step in range(4):
        rows = slice(step * 128, step * 128 + 128)
        scores = scores_of(projected[rows, 0:128], keys)
        weights = softmax(jnp.where(at_row == at_column, scores, -1e30))
        out[rows, :] = jnp.dot(weights, values, preferred_element_type=F32).astype(BF16)


def spatial_kernel(place, *refs):
    window, normed, out, weight, parts, projected, sem, sems = refs[8:]
    projected[...] = project(normed, weight, parts, sems, fetch(0, place, refs[:8], weight, sem))

    def tile_of(step, _):
        rows = pl.ds(pl.multiple_of(step * TILE, TILE), TILE)
        chosen = [pl.ds(pl.multiple_of(window[i, step] * TILE, TILE), TILE) for i in range(WIN)]
        keys = jnp.concatenate([projected[there, 128:256] for there in chosen], 0)
        values = jnp.concatenate([projected[there, 256:384] for there in chosen], 0)
        weights = softmax(scores_of(projected[rows, 0:128], keys))
        out[rows, :] = jnp.dot(weights, values, preferred_element_type=F32).astype(BF16)
        return 0

    lax.fori_loop(0, 8, tile_of, 0, unroll=True)


def heads_times(heads, w_out, wide, x, side):
    for j, ahead in enumerate((0, 3, 1, 2)):
        for kind in range(2):
            wide[:, (j * 2 + kind) * HD : (j * 2 + kind + 1) * HD] = heads[j, kind]
    rows = jnp.concatenate([w_out[(x + ahead) % 4 * 2 + side] for ahead in (0, 3, 1, 2)], 0)
    return jnp.dot(wide[...], rows, preferred_element_type=F32)


def share_kernel(place, heads, w_out, share, wide):
    share[...] = heads_times(heads, w_out, wide, place[2], place[3])


def mixed_kernel(place, heads, w_out, share, hidden, gate, out, wide):
    total = share[...] + heads_times(heads, w_out, wide, place[2], 1 - place[3])
    for k in range(3):
        columns = slice(k * 128, k * 128 + 128)
        scale = gate[pl.ds((place[2] * 2 + place[3]) * 3 + k, 1), :]
        out[:, columns] = (hidden[:, columns].astype(F32) + scale * total[:, columns]).astype(BF16)


def params(flops, size, limit=56):
    return dict(
        compiler_params=pltpu.CompilerParams(vmem_limit_bytes=limit * 1024 * 1024),
        cost_estimate=pl.CostEstimate(flops=flops, bytes_accessed=size, transcendentals=0),
    )


def body(hidden, shift_mod, scale_mod, gate, w_qkv, w_out, window_tiles):
    x, core, zl, yl = (lax.axis_index(name) for name in ("x", "c", "zl", "yl"))
    place = jnp.stack([yl, zl, x, core]).astype(jnp.int32)
    shift, scale, gate = (value.reshape(24, 128) for value in (shift_mod, scale_mod, gate))

    shards = jnp.concatenate([w_qkv[:, :, 0].reshape(96, 384), w_qkv[:, :, 1].reshape(96, 384)], 0)

    sent = pl.pallas_call(
        sent_kernel,
        out_shape=jax.ShapeDtypeStruct((8, 768, 384), BF16),
        in_specs=[VMEM, VMEM],
        out_specs=HBM,
        scratch_shapes=[pltpu.SemaphoreType.DMA((24,))],
        name="sent",
        **params(0, 7_000_000),
    )(hidden, w_out)
    arrived = lax.all_to_all(sent, ("x", "c"), split_axis=0, concat_axis=0, tiled=True)

    own = lax.all_gather(shards, "zh", axis=0)
    below, above = along_z(own, 1), along_z(own, -1)
    spatial_rows, temporal_rows = slice(0, 96), slice(96, 192)
    far_below, far_above = along_z(own[:2, temporal_rows], 2), along_z(own[2:, temporal_rows], -2)
    near_own = along_y(own, 1)
    place, own, below, above, far_below, near_own = tie(place, own, below, above, far_below, near_own)
    far_spatial = along_z(own[:, spatial_rows], 2)

    def near(rows, first, second):
        high = along_y(jnp.concatenate([above[:, rows], first], 0), -1)
        return along_y(jnp.concatenate([below[:, rows], second], 0), 1), high

    near_temporal = near(temporal_rows, far_below, far_above)
    temporal_weights = (own, below, above, far_below, far_above, near_own, *near_temporal)

    normed = pl.pallas_call(
        norm_kernel,
        out_shape=jax.ShapeDtypeStruct((512, D), BF16),
        grid=(4,),
        in_specs=[
            pl.BlockSpec((8, 128, 384), lambda i: (0, i, 0)),
            pl.BlockSpec((24, 128), lambda i: (0, 0)),
            pl.BlockSpec((24, 128), lambda i: (0, 0)),
        ],
        out_specs=pl.BlockSpec((128, D), lambda i: (i, 0)),
        name="norm",
        **params(20_000_000, 6_000_000),
    )(arrived, shift, scale)

    projected = pl.pallas_call(
        temporal_project_kernel,
        out_shape=jax.ShapeDtypeStruct((512, 384), BF16),
        in_specs=[SMEM] + [HBM] * 9,
        out_specs=VMEM,
        scratch_shapes=[
            pltpu.VMEM((8, 4, 96, 384), BF16),
            pltpu.VMEM((4, 512, 768), BF16),
            pltpu.SemaphoreType.DMA((10,)),
            pltpu.SemaphoreType.DMA((4,)),
        ],
        name="temporal_project",
        **params(1_200_000_000, 6_000_000),
    )(place, *temporal_weights, normed)
    projected, far_spatial = tie(projected, far_spatial)
    by_position = lax.all_to_all(
        projected.reshape(32, 16, 384), ("yl", "zh", "zl"), split_axis=0, concat_axis=0, tiled=True
    ).reshape(512, 384)

    below, above, far_spatial, _ = tie(below, above, far_spatial, projected)
    by_position, *near_spatial = tie(by_position, *near(spatial_rows, far_spatial[:2], far_spatial[2:]))
    spatial_weights = (own, below, above, far_spatial[:2], far_spatial[2:], near_own, *near_spatial)

    temporal = pl.pallas_call(
        temporal_kernel,
        out_shape=jax.ShapeDtypeStruct((512, HD), BF16),
        in_specs=[VMEM],
        out_specs=VMEM,
        name="temporal",
        **params(140_000_000, 500_000),
    )(by_position)
    temporal = lax.all_to_all(
        temporal.reshape(32, 16, HD), ("yl", "zh", "zl"), split_axis=0, concat_axis=0, tiled=True
    ).reshape(512, HD)
    spatial = pl.pallas_call(
        spatial_kernel,
        out_shape=jax.ShapeDtypeStruct((512, HD), BF16),
        in_specs=[SMEM] + [HBM] * 8 + [SMEM, HBM],
        out_specs=VMEM,
        scratch_shapes=[
            pltpu.VMEM((8, 4, 96, 384), BF16),
            pltpu.VMEM((4, 512, 768), BF16),
            pltpu.VMEM((512, 384), BF16),
            pltpu.SemaphoreType.DMA((10,)),
            pltpu.SemaphoreType.DMA((4,)),
        ],
        name="spatial",
        **params(1_300_000_000, 6_000_000),
    )(place, *spatial_weights, window_tiles.T, normed)

    heads = jnp.stack([spatial, temporal])
    mine = jnp.stack([heads, along_x(heads, 1), along_x(heads, -1), along_x(heads, 2)])
    theirs = other_core(mine)
    share = pl.pallas_call(
        share_kernel,
        out_shape=jax.ShapeDtypeStruct((512, 384), F32),
        grid=(2,),
        in_specs=[SMEM, HEADS, COLUMNS],
        out_specs=ROWS,
        scratch_shapes=[pltpu.VMEM((256, 1024), BF16)],
        name="share",
        **params(400_000_000, 4_000_000, 24),
    )(place, mine, arrived)
    return pl.pallas_call(
        mixed_kernel,
        out_shape=jax.ShapeDtypeStruct((512, 384), BF16),
        grid=(2,),
        in_specs=[SMEM, HEADS, COLUMNS, ROWS, ROWS, pl.BlockSpec((24, 128), lambda i: (0, 0))],
        out_specs=ROWS,
        scratch_shapes=[pltpu.VMEM((256, 1024), BF16)],
        name="mixed",
        **params(400_000_000, 5_000_000, 24),
    )(place, theirs, arrived, share, hidden, gate)


def solution(mesh):
    fine = Mesh(mesh.devices.reshape(2, 4, 4, 4, 2, 2), ("yl", "zh", "zl", "x", "c", "dp"))
    seq, tp = ("yl", "zh", "zl"), ("x", "c")
    in_specs = (
        P(("dp",) + seq, tp),
        P("dp"),
        P("dp"),
        P("dp"),
        P(seq, None, None, tp),
        P(None, tp, None),
        P(),
    )
    out_specs = P(("dp",) + seq, tp)
    return jax.shard_map(body, mesh=fine, in_specs=in_specs, out_specs=out_specs, check_vma=False)
```

```python
import functools

import jax
import jax.numpy as jnp
from jax import lax
from jax.experimental import pallas as pl
from jax.experimental.pallas import tpu as pltpu
from jax.sharding import Mesh, PartitionSpec as P

D = 3072
HD = 128
TILE = 64
WIN = 4
F32 = jnp.float32
BF16 = jnp.bfloat16
VMEM = pl.BlockSpec(memory_space=pltpu.VMEM)
SMEM = pl.BlockSpec(memory_space=pltpu.SMEM)
HBM = pl.BlockSpec(memory_space=pl.ANY)
COLUMNS = pl.BlockSpec((8, 256, 384), lambda i: (0, 2, 0))
ROWS = pl.BlockSpec((256, 384), lambda i: (i, 0))
HEADS = pl.BlockSpec((4, 2, 256, HD), lambda i: (0, 0, i, 0))

Y_PLACE = (0, 2, 1, 3)


def along_z(value, step):
    return lax.ppermute(value, ("zh", "zl"), [(i, (i + step) % 16) for i in range(16)])


def along_x(value, step):
    return lax.ppermute(value, "x", [(i, (i + step) % 4) for i in range(4)])


def along_y(value, step):
    return lax.ppermute(value, ("yl", "dp"), [(Y_PLACE[i], Y_PLACE[(i + step) % 4]) for i in range(4)])


def other_core(value):
    return lax.ppermute(value, "c", [(0, 1), (1, 0)])


def tie(*values):
    return lax.optimization_barrier(values)


def norm_kernel(blocks_ref, shift, scale, normed):
    def rows_of(step, _):
        rows = pl.ds(pl.multiple_of(step * 16, 16), 16)
        blocks = [blocks_ref[j, rows, :].astype(F32) for j in range(8)]
        middle = jnp.sum(sum(blocks), -1, keepdims=True) * (1.0 / D)
        blocks = [block - middle for block in blocks]
        spread = jnp.sum(sum(block * block for block in blocks), -1, keepdims=True) * (1.0 / D)
        inverse = lax.rsqrt(spread + 1e-06)
        for j in range(24):
            block = blocks[j // 3][:, j % 3 * 128 : j % 3 * 128 + 128]
            value = block * inverse * (1.0 + scale[j : j + 1, :]) + shift[j : j + 1, :]
            normed[rows, j * 128 : j * 128 + 128] = value.astype(BF16)
        return 0

    lax.fori_loop(0, normed.shape[0] // 16, rows_of, 0, unroll=4)


def project(normed, weight, parts, sems, fetched):
    copies = [pltpu.make_async_copy(normed.at[:, pl.ds(i * 768, 768)], parts.at[i], sems.at[i]) for i in range(4)]
    for copy in copies:
        copy.start()
    for copy in fetched:
        copy.wait()
    total = 0.0
    for i, copy in enumerate(copies):
        copy.wait()
        rows = weight[i * 2 : i * 2 + 2].reshape(768, 384)
        total += jnp.dot(parts[i], rows, preferred_element_type=F32)
    return total.astype(BF16)


def softmax(scores):
    raised = jnp.exp(scores - jnp.max(scores, -1, keepdims=True))
    return (raised * (1.0 / jnp.sum(raised, -1, keepdims=True))).astype(BF16)


def scores_of(queries, keys):
    return lax.dot_general(queries, keys, (((1,), (1,)), ((), ())), preferred_element_type=F32) * float(HD) ** (-0.5)


def sent_kernel(hidden, w_out, sent, hidden_here, w_out_here, sem, sems):
    loads = [pltpu.make_async_copy(hidden, hidden_here, sem.at[0]), pltpu.make_async_copy(w_out, w_out_here, sem.at[1])]
    for load in loads:
        load.start()
    copies = [pltpu.make_async_copy(hidden_here, sent.at[g, pl.ds(0, 512)], sems.at[g]) for g in range(8)]
    for g in range(8):
        for kind in range(2):
            columns = w_out_here.at[kind, :, pl.ds(g * 384, 384)]
            there = sent.at[g, pl.ds(512 + kind * HD, HD)]
            copies.append(pltpu.make_async_copy(columns, there, sems.at[len(copies)]))
    loads[0].wait()
    for copy in copies[:8]:
        copy.start()
    loads[1].wait()
    for copy in copies[8:]:
        copy.start()
    for copy in copies:
        copy.wait()


def fetch(kind, place, pieces, weight, sem):
    own, below, above, far_first, far_second, near_own, near_low, near_high = pieces
    own, below, above, near_own = (piece.at[:, pl.ds(kind * 96, 96)] for piece in (own, below, above, near_own))
    here, there = place[0] * 4, (1 - place[0]) * 4
    parts = (
        (own, here, 4, 0),
        (below, here, 4, 3),
        (above, here, 4, 1),
        (far_first, here, 2, 2),
        (far_second, here + 2, 2, 2),
        (near_own, there, 4, 0),
        (near_low.at[0:4], there, 4, 3),
        (near_low.at[4:6], there + 2, 2, 2),
        (near_high.at[0:4], there, 4, 1),
        (near_high.at[4:6], there, 2, 2),
    )
    copies = [
        pltpu.make_async_copy(part, weight.at[pl.ds(start, count), (place[1] + ahead) % 4], sem.at[i])
        for i, (part, start, count, ahead) in enumerate(parts)
    ]
    for copy in copies:
        copy.start()
    return copies


def temporal_project_kernel(place, *refs):
    normed, out, weight, parts, sem, sems = refs[8:]
    out[...] = project(normed, weight, parts, sems, fetch(1, place, refs[:8], weight, sem))


def temporal_kernel(projected, out):
    keys, values = projected[:, 128:256], projected[:, 256:384]
    at_row = lax.broadcasted_iota(jnp.int32, (128, 512), 0) % 16
    at_column = lax.broadcasted_iota(jnp.int32, (128, 512), 1) % 16
    for step in range(4):
        rows = slice(step * 128, step * 128 + 128)
        scores = scores_of(projected[rows, 0:128], keys)
        weights = softmax(jnp.where(at_row == at_column, scores, -1e30))
        out[rows, :] = jnp.dot(weights, values, preferred_element_type=F32).astype(BF16)


def spatial_kernel(place, *refs):
    window, normed, out, weight, parts, projected, sem, sems = refs[8:]
    projected[...] = project(normed, weight, parts, sems, fetch(0, place, refs[:8], weight, sem))

    def tile_of(step, _):
        rows = pl.ds(pl.multiple_of(step * TILE, TILE), TILE)
        chosen = [pl.ds(pl.multiple_of(window[i, step] * TILE, TILE), TILE) for i in range(WIN)]
        keys = jnp.concatenate([projected[there, 128:256] for there in chosen], 0)
        values = jnp.concatenate([projected[there, 256:384] for there in chosen], 0)
        weights = softmax(scores_of(projected[rows, 0:128], keys))
        out[rows, :] = jnp.dot(weights, values, preferred_element_type=F32).astype(BF16)
        return 0

    lax.fori_loop(0, 8, tile_of, 0, unroll=True)


def heads_times(heads, w_out, wide, x, side):
    for j, ahead in enumerate((0, 3, 1, 2)):
        for kind in range(2):
            wide[:, (j * 2 + kind) * HD : (j * 2 + kind + 1) * HD] = heads[j, kind]
    rows = jnp.concatenate([w_out[(x + ahead) % 4 * 2 + side] for ahead in (0, 3, 1, 2)], 0)
    return jnp.dot(wide[...], rows, preferred_element_type=F32)


def share_kernel(place, heads, w_out, share, wide):
    share[...] = heads_times(heads, w_out, wide, place[2], place[3])


def mixed_kernel(place, heads, w_out, share, hidden, gate, out, wide):
    total = share[...] + heads_times(heads, w_out, wide, place[2], 1 - place[3])
    for k in range(3):
        columns = slice(k * 128, k * 128 + 128)
        scale = gate[pl.ds((place[2] * 2 + place[3]) * 3 + k, 1), :]
        out[:, columns] = (hidden[:, columns].astype(F32) + scale * total[:, columns]).astype(BF16)


def params(flops, size, limit=56):
    return dict(
        compiler_params=pltpu.CompilerParams(vmem_limit_bytes=limit * 1024 * 1024),
        cost_estimate=pl.CostEstimate(flops=flops, bytes_accessed=size, transcendentals=0),
    )


def body(hidden, shift_mod, scale_mod, gate, w_qkv, w_out, window_tiles):
    x, core, zl, yl = (lax.axis_index(name) for name in ("x", "c", "zl", "yl"))
    place = jnp.stack([yl, zl, x, core]).astype(jnp.int32)
    shift, scale, gate = (value.reshape(24, 128) for value in (shift_mod, scale_mod, gate))

    shards = jnp.concatenate([w_qkv[:, :, 0].reshape(96, 384), w_qkv[:, :, 1].reshape(96, 384)], 0)

    sent = pl.pallas_call(
        sent_kernel,
        out_shape=jax.ShapeDtypeStruct((8, 768, 384), BF16),
        in_specs=[HBM, HBM],
        out_specs=HBM,
        scratch_shapes=[
            pltpu.VMEM((512, 384), BF16),
            pltpu.VMEM((2, HD, D), BF16),
            pltpu.SemaphoreType.DMA((2,)),
            pltpu.SemaphoreType.DMA((24,)),
        ],
        name="sent",
        **params(0, 7_000_000),
    )(hidden, w_out)
    arrived = lax.all_to_all(sent, ("x", "c"), split_axis=0, concat_axis=0, tiled=True)

    own = lax.all_gather(shards, "zh", axis=0)
    below, above = along_z(own, 1), along_z(own, -1)
    spatial_rows, temporal_rows = slice(0, 96), slice(96, 192)
    far_below, far_above = along_z(own[:2, temporal_rows], 2), along_z(own[2:, temporal_rows], -2)
    near_own = along_y(own, 1)
    place, own, below, above, far_below, near_own = tie(place, own, below, above, far_below, near_own)
    far_spatial = along_z(own[:, spatial_rows], 2)

    def near(rows, first, second):
        high = along_y(jnp.concatenate([above[:, rows], first], 0), -1)
        return along_y(jnp.concatenate([below[:, rows], second], 0), 1), high

    near_temporal = near(temporal_rows, far_below, far_above)
    temporal_weights = (own, below, above, far_below, far_above, near_own, *near_temporal)

    normed = pl.pallas_call(
        norm_kernel,
        out_shape=jax.ShapeDtypeStruct((512, D), BF16),
        grid=(4,),
        in_specs=[
            pl.BlockSpec((8, 128, 384), lambda i: (0, i, 0)),
            pl.BlockSpec((24, 128), lambda i: (0, 0)),
            pl.BlockSpec((24, 128), lambda i: (0, 0)),
        ],
        out_specs=pl.BlockSpec((128, D), lambda i: (i, 0)),
        name="norm",
        **params(20_000_000, 6_000_000),
    )(arrived, shift, scale)

    projected = pl.pallas_call(
        temporal_project_kernel,
        out_shape=jax.ShapeDtypeStruct((512, 384), BF16),
        in_specs=[SMEM] + [HBM] * 9,
        out_specs=VMEM,
        scratch_shapes=[
            pltpu.VMEM((8, 4, 96, 384), BF16),
            pltpu.VMEM((4, 512, 768), BF16),
            pltpu.SemaphoreType.DMA((10,)),
            pltpu.SemaphoreType.DMA((4,)),
        ],
        name="temporal_project",
        **params(1_200_000_000, 6_000_000),
    )(place, *temporal_weights, normed)
    projected, far_spatial = tie(projected, far_spatial)
    by_position = lax.all_to_all(
        projected.reshape(32, 16, 384), ("yl", "zh", "zl"), split_axis=0, concat_axis=0, tiled=True
    ).reshape(512, 384)

    below, above, far_spatial, _ = tie(below, above, far_spatial, projected)
    by_position, *near_spatial = tie(by_position, *near(spatial_rows, far_spatial[:2], far_spatial[2:]))
    spatial_weights = (own, below, above, far_spatial[:2], far_spatial[2:], near_own, *near_spatial)

    temporal = pl.pallas_call(
        temporal_kernel,
        out_shape=jax.ShapeDtypeStruct((512, HD), BF16),
        in_specs=[VMEM],
        out_specs=VMEM,
        name="temporal",
        **params(140_000_000, 500_000, 24),
    )(by_position)
    temporal = lax.all_to_all(
        temporal.reshape(32, 16, HD), ("yl", "zh", "zl"), split_axis=0, concat_axis=0, tiled=True
    ).reshape(512, HD)
    spatial = pl.pallas_call(
        spatial_kernel,
        out_shape=jax.ShapeDtypeStruct((512, HD), BF16),
        in_specs=[SMEM] + [HBM] * 8 + [SMEM, HBM],
        out_specs=VMEM,
        scratch_shapes=[
            pltpu.VMEM((8, 4, 96, 384), BF16),
            pltpu.VMEM((4, 512, 768), BF16),
            pltpu.VMEM((512, 384), BF16),
            pltpu.SemaphoreType.DMA((10,)),
            pltpu.SemaphoreType.DMA((4,)),
        ],
        name="spatial",
        **params(1_300_000_000, 6_000_000),
    )(place, *spatial_weights, window_tiles.T, normed)

    heads = jnp.stack([spatial, temporal])
    mine = jnp.stack([heads, along_x(heads, 1), along_x(heads, -1), along_x(heads, 2)])
    theirs = other_core(mine)
    share = pl.pallas_call(
        share_kernel,
        out_shape=jax.ShapeDtypeStruct((512, 384), F32),
        grid=(2,),
        in_specs=[SMEM, HEADS, COLUMNS],
        out_specs=ROWS,
        scratch_shapes=[pltpu.VMEM((256, 1024), BF16)],
        name="share",
        **params(400_000_000, 4_000_000, 24),
    )(place, mine, arrived)
    return pl.pallas_call(
        mixed_kernel,
        out_shape=jax.ShapeDtypeStruct((512, 384), BF16),
        grid=(2,),
        in_specs=[SMEM, HEADS, COLUMNS, ROWS, ROWS, pl.BlockSpec((24, 128), lambda i: (0, 0))],
        out_specs=ROWS,
        scratch_shapes=[pltpu.VMEM((256, 1024), BF16)],
        name="mixed",
        **params(400_000_000, 5_000_000, 24),
    )(place, theirs, arrived, share, hidden, gate)


def solution(mesh):
    fine = Mesh(mesh.devices.reshape(2, 4, 4, 4, 2, 2), ("yl", "zh", "zl", "x", "c", "dp"))
    seq, tp = ("yl", "zh", "zl"), ("x", "c")
    in_specs = (
        P(("dp",) + seq, tp),
        P("dp"),
        P("dp"),
        P("dp"),
        P(seq, None, None, tp),
        P(None, tp, None),
        P(),
    )
    out_specs = P(("dp",) + seq, tp)
    return jax.shard_map(body, mesh=fine, in_specs=in_specs, out_specs=out_specs, check_vma=False)
```

```python
import functools

import jax
import jax.numpy as jnp
from jax import lax
from jax.experimental import pallas as pl
from jax.experimental.pallas import tpu as pltpu
from jax.sharding import Mesh, PartitionSpec as P

D = 3072
HD = 128
TILE = 64
WIN = 4
F32 = jnp.float32
BF16 = jnp.bfloat16
VMEM = pl.BlockSpec(memory_space=pltpu.VMEM)
SMEM = pl.BlockSpec(memory_space=pltpu.SMEM)
HBM = pl.BlockSpec(memory_space=pl.ANY)
COLUMNS = pl.BlockSpec((8, 256, 384), lambda i: (0, 2, 0))
ROWS = pl.BlockSpec((512, 384), lambda i: (i, 0))
HEADS = pl.BlockSpec((4, 2, 512, HD), lambda i: (0, 0, i, 0))

Y_PLACE = (0, 2, 1, 3)


def along_z(value, step):
    return lax.ppermute(value, ("zh", "zl"), [(i, (i + step) % 16) for i in range(16)])


def along_x(value, step):
    return lax.ppermute(value, "x", [(i, (i + step) % 4) for i in range(4)])


def along_y(value, step):
    return lax.ppermute(value, ("yl", "dp"), [(Y_PLACE[i], Y_PLACE[(i + step) % 4]) for i in range(4)])


def other_core(value):
    return lax.ppermute(value, "c", [(0, 1), (1, 0)])


def tie(*values):
    return lax.optimization_barrier(values)


def norm_kernel(blocks_ref, shift, scale, normed):
    def rows_of(step, _):
        rows = pl.ds(pl.multiple_of(step * 16, 16), 16)
        blocks = [blocks_ref[j, rows, :].astype(F32) for j in range(8)]
        middle = jnp.sum(sum(blocks), -1, keepdims=True) * (1.0 / D)
        blocks = [block - middle for block in blocks]
        spread = jnp.sum(sum(block * block for block in blocks), -1, keepdims=True) * (1.0 / D)
        inverse = lax.rsqrt(spread + 1e-06)
        for j in range(24):
            block = blocks[j // 3][:, j % 3 * 128 : j % 3 * 128 + 128]
            value = block * inverse * (1.0 + scale[j : j + 1, :]) + shift[j : j + 1, :]
            normed[rows, j * 128 : j * 128 + 128] = value.astype(BF16)
        return 0

    lax.fori_loop(0, normed.shape[0] // 16, rows_of, 0, unroll=4)


def project(normed, weight, parts, sems, fetched):
    copies = [pltpu.make_async_copy(normed.at[:, pl.ds(i * 768, 768)], parts.at[i], sems.at[i]) for i in range(4)]
    for copy in copies:
        copy.start()
    for copy in fetched:
        copy.wait()
    total = 0.0
    for i, copy in enumerate(copies):
        copy.wait()
        rows = weight[i * 2 : i * 2 + 2].reshape(768, 384)
        total += jnp.dot(parts[i], rows, preferred_element_type=F32)
    return total.astype(BF16)


def softmax(scores):
    raised = jnp.exp(scores - jnp.max(scores, -1, keepdims=True))
    return (raised * (1.0 / jnp.sum(raised, -1, keepdims=True))).astype(BF16)


def scores_of(queries, keys):
    return lax.dot_general(queries, keys, (((1,), (1,)), ((), ())), preferred_element_type=F32) * float(HD) ** (-0.5)


def sent_kernel(hidden, w_out, sent, hidden_here, w_out_here, sem, sems):
    loads = [pltpu.make_async_copy(hidden, hidden_here, sem.at[0]), pltpu.make_async_copy(w_out, w_out_here, sem.at[1])]
    for load in loads:
        load.start()
    copies = [pltpu.make_async_copy(hidden_here, sent.at[g, pl.ds(0, 512)], sems.at[g]) for g in range(8)]
    for g in range(8):
        for kind in range(2):
            columns = w_out_here.at[kind, :, pl.ds(g * 384, 384)]
            there = sent.at[g, pl.ds(512 + kind * HD, HD)]
            copies.append(pltpu.make_async_copy(columns, there, sems.at[len(copies)]))
    loads[0].wait()
    for copy in copies[:8]:
        copy.start()
    loads[1].wait()
    for copy in copies[8:]:
        copy.start()
    for copy in copies:
        copy.wait()


def fetch(kind, place, pieces, weight, sem):
    own, below, above, far_first, far_second, near_own, near_low, near_high = pieces
    own, below, above, near_own = (piece.at[:, pl.ds(kind * 96, 96)] for piece in (own, below, above, near_own))
    here, there = place[0] * 4, (1 - place[0]) * 4
    parts = (
        (own, here, 4, 0),
        (below, here, 4, 3),
        (above, here, 4, 1),
        (far_first, here, 2, 2),
        (far_second, here + 2, 2, 2),
        (near_own, there, 4, 0),
        (near_low.at[0:4], there, 4, 3),
        (near_low.at[4:6], there + 2, 2, 2),
        (near_high.at[0:4], there, 4, 1),
        (near_high.at[4:6], there, 2, 2),
    )
    copies = [
        pltpu.make_async_copy(part, weight.at[pl.ds(start, count), (place[1] + ahead) % 4], sem.at[i])
        for i, (part, start, count, ahead) in enumerate(parts)
    ]
    for copy in copies:
        copy.start()
    return copies


def temporal_project_kernel(place, *refs):
    normed, out, weight, parts, sem, sems = refs[8:]
    out[...] = project(normed, weight, parts, sems, fetch(1, place, refs[:8], weight, sem))


def temporal_kernel(projected, out):
    keys, values = projected[:, 128:256], projected[:, 256:384]
    at_row = lax.broadcasted_iota(jnp.int32, (128, 512), 0) % 16
    at_column = lax.broadcasted_iota(jnp.int32, (128, 512), 1) % 16
    for step in range(4):
        rows = slice(step * 128, step * 128 + 128)
        scores = scores_of(projected[rows, 0:128], keys)
        weights = softmax(jnp.where(at_row == at_column, scores, -1e30))
        out[rows, :] = jnp.dot(weights, values, preferred_element_type=F32).astype(BF16)


def spatial_kernel(place, *refs):
    window, normed, out, weight, parts, projected, sem, sems = refs[8:]
    projected[...] = project(normed, weight, parts, sems, fetch(0, place, refs[:8], weight, sem))

    def tile_of(step, _):
        rows = pl.ds(pl.multiple_of(step * TILE, TILE), TILE)
        chosen = [pl.ds(pl.multiple_of(window[i, step] * TILE, TILE), TILE) for i in range(WIN)]
        keys = jnp.concatenate([projected[there, 128:256] for there in chosen], 0)
        values = jnp.concatenate([projected[there, 256:384] for there in chosen], 0)
        weights = softmax(scores_of(projected[rows, 0:128], keys))
        out[rows, :] = jnp.dot(weights, values, preferred_element_type=F32).astype(BF16)
        return 0

    lax.fori_loop(0, 8, tile_of, 0, unroll=True)


def heads_times(heads, w_out, wide, x, side):
    for j, ahead in enumerate((0, 3, 1, 2)):
        for kind in range(2):
            wide[:, (j * 2 + kind) * HD : (j * 2 + kind + 1) * HD] = heads[j, kind]
    rows = jnp.concatenate([w_out[(x + ahead) % 4 * 2 + side] for ahead in (0, 3, 1, 2)], 0)
    return jnp.dot(wide[...], rows, preferred_element_type=F32)


def share_kernel(place, heads, w_out, share, wide):
    share[...] = heads_times(heads, w_out, wide, place[2], place[3])


def mixed_kernel(place, heads, w_out, share, hidden, gate, out, wide):
    total = share[...] + heads_times(heads, w_out, wide, place[2], 1 - place[3])
    for k in range(3):
        columns = slice(k * 128, k * 128 + 128)
        scale = gate[pl.ds((place[2] * 2 + place[3]) * 3 + k, 1), :]
        out[:, columns] = (hidden[:, columns].astype(F32) + scale * total[:, columns]).astype(BF16)


def params(flops, size, limit=56):
    return dict(
        compiler_params=pltpu.CompilerParams(vmem_limit_bytes=limit * 1024 * 1024),
        cost_estimate=pl.CostEstimate(flops=flops, bytes_accessed=size, transcendentals=0),
    )


def body(hidden, shift_mod, scale_mod, gate, w_qkv, w_out, window_tiles):
    x, core, zl, yl = (lax.axis_index(name) for name in ("x", "c", "zl", "yl"))
    place = jnp.stack([yl, zl, x, core]).astype(jnp.int32)
    shift, scale, gate = (value.reshape(24, 128) for value in (shift_mod, scale_mod, gate))

    shards = jnp.concatenate([w_qkv[:, :, 0].reshape(96, 384), w_qkv[:, :, 1].reshape(96, 384)], 0)

    sent = pl.pallas_call(
        sent_kernel,
        out_shape=jax.ShapeDtypeStruct((8, 768, 384), BF16),
        in_specs=[HBM, HBM],
        out_specs=HBM,
        scratch_shapes=[
            pltpu.VMEM((512, 384), BF16),
            pltpu.VMEM((2, HD, D), BF16),
            pltpu.SemaphoreType.DMA((2,)),
            pltpu.SemaphoreType.DMA((24,)),
        ],
        name="sent",
        **params(0, 7_000_000),
    )(hidden, w_out)
    arrived = lax.all_to_all(sent, ("x", "c"), split_axis=0, concat_axis=0, tiled=True)

    own = lax.all_gather(shards, "zh", axis=0)
    below, above = along_z(own, 1), along_z(own, -1)
    spatial_rows, temporal_rows = slice(0, 96), slice(96, 192)
    far_below, far_above = along_z(own[:2, temporal_rows], 2), along_z(own[2:, temporal_rows], -2)
    near_own = along_y(own, 1)
    place, own, below, above, far_below, near_own = tie(place, own, below, above, far_below, near_own)
    far_spatial = along_z(own[:, spatial_rows], 2)

    def near(rows, first, second):
        high = along_y(jnp.concatenate([above[:, rows], first], 0), -1)
        return along_y(jnp.concatenate([below[:, rows], second], 0), 1), high

    near_temporal = near(temporal_rows, far_below, far_above)
    temporal_weights = (own, below, above, far_below, far_above, near_own, *near_temporal)

    normed = pl.pallas_call(
        norm_kernel,
        out_shape=jax.ShapeDtypeStruct((512, D), BF16),
        grid=(2,),
        in_specs=[
            pl.BlockSpec((8, 256, 384), lambda i: (0, i, 0)),
            pl.BlockSpec((24, 128), lambda i: (0, 0)),
            pl.BlockSpec((24, 128), lambda i: (0, 0)),
        ],
        out_specs=pl.BlockSpec((256, D), lambda i: (i, 0)),
        name="norm",
        **params(20_000_000, 6_000_000),
    )(arrived, shift, scale)

    projected = pl.pallas_call(
        temporal_project_kernel,
        out_shape=jax.ShapeDtypeStruct((512, 384), BF16),
        in_specs=[SMEM] + [HBM] * 9,
        out_specs=VMEM,
        scratch_shapes=[
            pltpu.VMEM((8, 4, 96, 384), BF16),
            pltpu.VMEM((4, 512, 768), BF16),
            pltpu.SemaphoreType.DMA((10,)),
            pltpu.SemaphoreType.DMA((4,)),
        ],
        name="temporal_project",
        **params(1_200_000_000, 6_000_000),
    )(place, *temporal_weights, normed)
    projected, far_spatial = tie(projected, far_spatial)
    by_position = lax.all_to_all(
        projected.reshape(32, 16, 384), ("yl", "zh", "zl"), split_axis=0, concat_axis=0, tiled=True
    ).reshape(512, 384)

    below, above, far_spatial, _ = tie(below, above, far_spatial, projected)
    by_position, *near_spatial = tie(by_position, *near(spatial_rows, far_spatial[:2], far_spatial[2:]))
    spatial_weights = (own, below, above, far_spatial[:2], far_spatial[2:], near_own, *near_spatial)

    temporal = pl.pallas_call(
        temporal_kernel,
        out_shape=jax.ShapeDtypeStruct((512, HD), BF16),
        in_specs=[VMEM],
        out_specs=VMEM,
        name="temporal",
        **params(140_000_000, 500_000, 24),
    )(by_position)
    temporal = lax.all_to_all(
        temporal.reshape(32, 16, HD), ("yl", "zh", "zl"), split_axis=0, concat_axis=0, tiled=True
    ).reshape(512, HD)
    spatial = pl.pallas_call(
        spatial_kernel,
        out_shape=jax.ShapeDtypeStruct((512, HD), BF16),
        in_specs=[SMEM] + [HBM] * 8 + [SMEM, HBM],
        out_specs=VMEM,
        scratch_shapes=[
            pltpu.VMEM((8, 4, 96, 384), BF16),
            pltpu.VMEM((4, 512, 768), BF16),
            pltpu.VMEM((512, 384), BF16),
            pltpu.SemaphoreType.DMA((10,)),
            pltpu.SemaphoreType.DMA((4,)),
        ],
        name="spatial",
        **params(1_300_000_000, 6_000_000),
    )(place, *spatial_weights, window_tiles.T, normed)

    heads = jnp.stack([spatial, temporal])
    mine = jnp.stack([heads, along_x(heads, 1), along_x(heads, -1), along_x(heads, 2)])
    theirs = other_core(mine)
    share = pl.pallas_call(
        share_kernel,
        out_shape=jax.ShapeDtypeStruct((512, 384), F32),
        grid=(1,),
        in_specs=[SMEM, HEADS, COLUMNS],
        out_specs=ROWS,
        scratch_shapes=[pltpu.VMEM((512, 1024), BF16)],
        name="share",
        **params(400_000_000, 4_000_000, 24),
    )(place, mine, arrived)
    return pl.pallas_call(
        mixed_kernel,
        out_shape=jax.ShapeDtypeStruct((512, 384), BF16),
        grid=(1,),
        in_specs=[SMEM, HEADS, COLUMNS, ROWS, ROWS, pl.BlockSpec((24, 128), lambda i: (0, 0))],
        out_specs=ROWS,
        scratch_shapes=[pltpu.VMEM((512, 1024), BF16)],
        name="mixed",
        **params(400_000_000, 5_000_000, 24),
    )(place, theirs, arrived, share, hidden, gate)


def solution(mesh):
    fine = Mesh(mesh.devices.reshape(2, 4, 4, 4, 2, 2), ("yl", "zh", "zl", "x", "c", "dp"))
    seq, tp = ("yl", "zh", "zl"), ("x", "c")
    in_specs = (
        P(("dp",) + seq, tp),
        P("dp"),
        P("dp"),
        P("dp"),
        P(seq, None, None, tp),
        P(None, tp, None),
        P(),
    )
    out_specs = P(("dp",) + seq, tp)
    return jax.shard_map(body, mesh=fine, in_specs=in_specs, out_specs=out_specs, check_vma=False)
```

```python
import functools

import jax
import jax.numpy as jnp
from jax import lax
from jax.experimental import pallas as pl
from jax.experimental.pallas import tpu as pltpu
from jax.sharding import Mesh, PartitionSpec as P

D = 3072
HD = 128
TILE = 64
WIN = 4
F32 = jnp.float32
BF16 = jnp.bfloat16
VMEM = pl.BlockSpec(memory_space=pltpu.VMEM)
SMEM = pl.BlockSpec(memory_space=pltpu.SMEM)
HBM = pl.BlockSpec(memory_space=pl.ANY)
COLUMNS = pl.BlockSpec((8, 256, 384), lambda i: (0, 2, 0))
ROWS = pl.BlockSpec((512, 384), lambda i: (i, 0))
HEADS = pl.BlockSpec((4, 2, 512, HD), lambda i: (0, 0, i, 0))

Y_PLACE = (0, 2, 1, 3)


def along_z(value, step):
    return lax.ppermute(value, ("zh", "zl"), [(i, (i + step) % 16) for i in range(16)])


def along_x(value, step):
    return lax.ppermute(value, "x", [(i, (i + step) % 4) for i in range(4)])


def along_y(value, step):
    return lax.ppermute(value, ("yl", "dp"), [(Y_PLACE[i], Y_PLACE[(i + step) % 4]) for i in range(4)])


def other_core(value):
    return lax.ppermute(value, "c", [(0, 1), (1, 0)])


def tie(*values):
    return lax.optimization_barrier(values)


def norm_kernel(blocks_ref, shift, scale, normed):
    def rows_of(step, _):
        rows = pl.ds(pl.multiple_of(step * 16, 16), 16)
        blocks = [blocks_ref[j, rows, :].astype(F32) for j in range(8)]
        middle = jnp.sum(sum(blocks), -1, keepdims=True) * (1.0 / D)
        blocks = [block - middle for block in blocks]
        spread = jnp.sum(sum(block * block for block in blocks), -1, keepdims=True) * (1.0 / D)
        inverse = lax.rsqrt(spread + 1e-06)
        for j in range(24):
            block = blocks[j // 3][:, j % 3 * 128 : j % 3 * 128 + 128]
            value = block * inverse * (1.0 + scale[j : j + 1, :]) + shift[j : j + 1, :]
            normed[rows, j * 128 : j * 128 + 128] = value.astype(BF16)
        return 0

    lax.fori_loop(0, normed.shape[0] // 16, rows_of, 0, unroll=8)


def project(normed, weight, parts, sems, fetched):
    copies = [pltpu.make_async_copy(normed.at[:, pl.ds(i * 768, 768)], parts.at[i], sems.at[i]) for i in range(4)]
    for copy in copies:
        copy.start()
    for copy in fetched:
        copy.wait()
    total = 0.0
    for i, copy in enumerate(copies):
        copy.wait()
        rows = weight[i * 2 : i * 2 + 2].reshape(768, 384)
        total += jnp.dot(parts[i], rows, preferred_element_type=F32)
    return total.astype(BF16)


def softmax(scores):
    raised = jnp.exp(scores - jnp.max(scores, -1, keepdims=True))
    return (raised * (1.0 / jnp.sum(raised, -1, keepdims=True))).astype(BF16)


def scores_of(queries, keys):
    return lax.dot_general(queries, keys, (((1,), (1,)), ((), ())), preferred_element_type=F32) * float(HD) ** (-0.5)


def sent_kernel(hidden, w_out, sent, hidden_here, w_out_here, sem, sems):
    loads = [pltpu.make_async_copy(hidden, hidden_here, sem.at[0]), pltpu.make_async_copy(w_out, w_out_here, sem.at[1])]
    for load in loads:
        load.start()
    copies = [pltpu.make_async_copy(hidden_here, sent.at[g, pl.ds(0, 512)], sems.at[g]) for g in range(8)]
    for g in range(8):
        for kind in range(2):
            columns = w_out_here.at[kind, :, pl.ds(g * 384, 384)]
            there = sent.at[g, pl.ds(512 + kind * HD, HD)]
            copies.append(pltpu.make_async_copy(columns, there, sems.at[len(copies)]))
    loads[0].wait()
    for copy in copies[:8]:
        copy.start()
    loads[1].wait()
    for copy in copies[8:]:
        copy.start()
    for copy in copies:
        copy.wait()


def fetch(kind, place, pieces, weight, sem):
    own, below, above, far_first, far_second, near_own, near_low, near_high = pieces
    own, below, above, near_own = (piece.at[:, pl.ds(kind * 96, 96)] for piece in (own, below, above, near_own))
    here, there = place[0] * 4, (1 - place[0]) * 4
    parts = (
        (own, here, 4, 0),
        (below, here, 4, 3),
        (above, here, 4, 1),
        (far_first, here, 2, 2),
        (far_second, here + 2, 2, 2),
        (near_own, there, 4, 0),
        (near_low.at[0:4], there, 4, 3),
        (near_low.at[4:6], there + 2, 2, 2),
        (near_high.at[0:4], there, 4, 1),
        (near_high.at[4:6], there, 2, 2),
    )
    copies = [
        pltpu.make_async_copy(part, weight.at[pl.ds(start, count), (place[1] + ahead) % 4], sem.at[i])
        for i, (part, start, count, ahead) in enumerate(parts)
    ]
    for copy in copies:
        copy.start()
    return copies


def temporal_project_kernel(place, *refs):
    normed, out, weight, parts, sem, sems = refs[8:]
    out[...] = project(normed, weight, parts, sems, fetch(1, place, refs[:8], weight, sem))


def temporal_kernel(projected, out):
    keys, values = projected[:, 128:256], projected[:, 256:384]
    at_row = lax.broadcasted_iota(jnp.int32, (128, 512), 0) % 16
    at_column = lax.broadcasted_iota(jnp.int32, (128, 512), 1) % 16
    for step in range(4):
        rows = slice(step * 128, step * 128 + 128)
        scores = scores_of(projected[rows, 0:128], keys)
        weights = softmax(jnp.where(at_row == at_column, scores, -1e30))
        out[rows, :] = jnp.dot(weights, values, preferred_element_type=F32).astype(BF16)


def spatial_kernel(place, *refs):
    window, normed, out, weight, parts, projected, sem, sems = refs[8:]
    projected[...] = project(normed, weight, parts, sems, fetch(0, place, refs[:8], weight, sem))

    def tile_of(step, _):
        rows = pl.ds(pl.multiple_of(step * TILE, TILE), TILE)
        chosen = [pl.ds(pl.multiple_of(window[i, step] * TILE, TILE), TILE) for i in range(WIN)]
        keys = jnp.concatenate([projected[there, 128:256] for there in chosen], 0)
        values = jnp.concatenate([projected[there, 256:384] for there in chosen], 0)
        weights = softmax(scores_of(projected[rows, 0:128], keys))
        out[rows, :] = jnp.dot(weights, values, preferred_element_type=F32).astype(BF16)
        return 0

    lax.fori_loop(0, 8, tile_of, 0, unroll=True)


def heads_times(heads, w_out, wide, x, side):
    for j, ahead in enumerate((0, 3, 1, 2)):
        for kind in range(2):
            wide[:, (j * 2 + kind) * HD : (j * 2 + kind + 1) * HD] = heads[j, kind]
    rows = jnp.concatenate([w_out[(x + ahead) % 4 * 2 + side] for ahead in (0, 3, 1, 2)], 0)
    return jnp.dot(wide[...], rows, preferred_element_type=F32)


def share_kernel(place, heads, w_out, share, wide):
    share[...] = heads_times(heads, w_out, wide, place[2], place[3])


def mixed_kernel(place, heads, w_out, share, hidden, gate, out, wide):
    total = share[...] + heads_times(heads, w_out, wide, place[2], 1 - place[3])
    for k in range(3):
        columns = slice(k * 128, k * 128 + 128)
        scale = gate[pl.ds((place[2] * 2 + place[3]) * 3 + k, 1), :]
        out[:, columns] = (hidden[:, columns].astype(F32) + scale * total[:, columns]).astype(BF16)


def params(flops, size, limit=56):
    return dict(
        compiler_params=pltpu.CompilerParams(vmem_limit_bytes=limit * 1024 * 1024),
        cost_estimate=pl.CostEstimate(flops=flops, bytes_accessed=size, transcendentals=0),
    )


def body(hidden, shift_mod, scale_mod, gate, w_qkv, w_out, window_tiles):
    x, core, zl, yl = (lax.axis_index(name) for name in ("x", "c", "zl", "yl"))
    place = jnp.stack([yl, zl, x, core]).astype(jnp.int32)
    shift, scale, gate = (value.reshape(24, 128) for value in (shift_mod, scale_mod, gate))

    shards = jnp.concatenate([w_qkv[:, :, 0].reshape(96, 384), w_qkv[:, :, 1].reshape(96, 384)], 0)

    sent = pl.pallas_call(
        sent_kernel,
        out_shape=jax.ShapeDtypeStruct((8, 768, 384), BF16),
        in_specs=[HBM, HBM],
        out_specs=HBM,
        scratch_shapes=[
            pltpu.VMEM((512, 384), BF16),
            pltpu.VMEM((2, HD, D), BF16),
            pltpu.SemaphoreType.DMA((2,)),
            pltpu.SemaphoreType.DMA((24,)),
        ],
        name="sent",
        **params(0, 7_000_000),
    )(hidden, w_out)
    arrived = lax.all_to_all(sent, ("x", "c"), split_axis=0, concat_axis=0, tiled=True)

    own = lax.all_gather(shards, "zh", axis=0)
    below, above = along_z(own, 1), along_z(own, -1)
    spatial_rows, temporal_rows = slice(0, 96), slice(96, 192)
    far_below, far_above = along_z(own[:2, temporal_rows], 2), along_z(own[2:, temporal_rows], -2)
    near_own = along_y(own, 1)
    place, own, below, above, far_below, near_own = tie(place, own, below, above, far_below, near_own)
    far_spatial = along_z(own[:, spatial_rows], 2)

    def near(rows, first, second):
        high = along_y(jnp.concatenate([above[:, rows], first], 0), -1)
        return along_y(jnp.concatenate([below[:, rows], second], 0), 1), high

    near_temporal = near(temporal_rows, far_below, far_above)
    temporal_weights = (own, below, above, far_below, far_above, near_own, *near_temporal)

    normed = pl.pallas_call(
        norm_kernel,
        out_shape=jax.ShapeDtypeStruct((512, D), BF16),
        grid=(2,),
        in_specs=[
            pl.BlockSpec((8, 256, 384), lambda i: (0, i, 0)),
            pl.BlockSpec((24, 128), lambda i: (0, 0)),
            pl.BlockSpec((24, 128), lambda i: (0, 0)),
        ],
        out_specs=pl.BlockSpec((256, D), lambda i: (i, 0)),
        name="norm",
        **params(20_000_000, 6_000_000),
    )(arrived, shift, scale)

    projected = pl.pallas_call(
        temporal_project_kernel,
        out_shape=jax.ShapeDtypeStruct((512, 384), BF16),
        in_specs=[SMEM] + [HBM] * 9,
        out_specs=VMEM,
        scratch_shapes=[
            pltpu.VMEM((8, 4, 96, 384), BF16),
            pltpu.VMEM((4, 512, 768), BF16),
            pltpu.SemaphoreType.DMA((10,)),
            pltpu.SemaphoreType.DMA((4,)),
        ],
        name="temporal_project",
        **params(1_200_000_000, 6_000_000),
    )(place, *temporal_weights, normed)
    projected, far_spatial = tie(projected, far_spatial)
    by_position = lax.all_to_all(
        projected.reshape(32, 16, 384), ("yl", "zh", "zl"), split_axis=0, concat_axis=0, tiled=True
    ).reshape(512, 384)

    below, above, far_spatial, _ = tie(below, above, far_spatial, projected)
    by_position, *near_spatial = tie(by_position, *near(spatial_rows, far_spatial[:2], far_spatial[2:]))
    spatial_weights = (own, below, above, far_spatial[:2], far_spatial[2:], near_own, *near_spatial)

    temporal = pl.pallas_call(
        temporal_kernel,
        out_shape=jax.ShapeDtypeStruct((512, HD), BF16),
        in_specs=[VMEM],
        out_specs=VMEM,
        name="temporal",
        **params(140_000_000, 500_000, 24),
    )(by_position)
    temporal = lax.all_to_all(
        temporal.reshape(32, 16, HD), ("yl", "zh", "zl"), split_axis=0, concat_axis=0, tiled=True
    ).reshape(512, HD)
    spatial = pl.pallas_call(
        spatial_kernel,
        out_shape=jax.ShapeDtypeStruct((512, HD), BF16),
        in_specs=[SMEM] + [HBM] * 8 + [SMEM, HBM],
        out_specs=VMEM,
        scratch_shapes=[
            pltpu.VMEM((8, 4, 96, 384), BF16),
            pltpu.VMEM((4, 512, 768), BF16),
            pltpu.VMEM((512, 384), BF16),
            pltpu.SemaphoreType.DMA((10,)),
            pltpu.SemaphoreType.DMA((4,)),
        ],
        name="spatial",
        **params(1_300_000_000, 6_000_000),
    )(place, *spatial_weights, window_tiles.T, normed)

    heads = jnp.stack([spatial, temporal])
    mine = jnp.stack([heads, along_x(heads, 1), along_x(heads, -1), along_x(heads, 2)])
    theirs = other_core(mine)
    share = pl.pallas_call(
        share_kernel,
        out_shape=jax.ShapeDtypeStruct((512, 384), F32),
        grid=(1,),
        in_specs=[SMEM, HEADS, COLUMNS],
        out_specs=ROWS,
        scratch_shapes=[pltpu.VMEM((512, 1024), BF16)],
        name="share",
        **params(400_000_000, 4_000_000, 24),
    )(place, mine, arrived)
    return pl.pallas_call(
        mixed_kernel,
        out_shape=jax.ShapeDtypeStruct((512, 384), BF16),
        grid=(1,),
        in_specs=[SMEM, HEADS, COLUMNS, ROWS, ROWS, pl.BlockSpec((24, 128), lambda i: (0, 0))],
        out_specs=ROWS,
        scratch_shapes=[pltpu.VMEM((512, 1024), BF16)],
        name="mixed",
        **params(400_000_000, 5_000_000, 24),
    )(place, theirs, arrived, share, hidden, gate)


def solution(mesh):
    fine = Mesh(mesh.devices.reshape(2, 4, 4, 4, 2, 2), ("yl", "zh", "zl", "x", "c", "dp"))
    seq, tp = ("yl", "zh", "zl"), ("x", "c")
    in_specs = (
        P(("dp",) + seq, tp),
        P("dp"),
        P("dp"),
        P("dp"),
        P(seq, None, None, tp),
        P(None, tp, None),
        P(),
    )
    out_specs = P(("dp",) + seq, tp)
    return jax.shard_map(body, mesh=fine, in_specs=in_specs, out_specs=out_specs, check_vma=False)
```
